128 devices in a mesh: dp: 16 (over z_hi, x, core), seq: 8 (over z_lo, y).
Axes of the slice: x: 4, y: 4, z: 4 (z_hi: 2, z_lo: 2; z = z_hi * 2 + z_lo), core: 2. Of those that a mesh axis runs over, the one named last changes fastest.
Arguments:
- queries: bfloat16 [16, 1024, 12288], P('dp', 'seq'), may hold values from -10 to 10
- latents: bfloat16 [16, 1024, 576], P('dp', 'seq'), may hold values from -6 to 6
- kv_weight: bfloat16 [512, 16384], P(None, 'seq'), may hold values from -0.25 to 0.25
- out_grad: bfloat16 [16, 1024, 8192], P('dp', 'seq'), may hold values from -6 to 6
Outputs:
- query_grad: bfloat16 [16, 1024, 12288], P('dp', 'seq')
- latent_grad: bfloat16 [16, 1024, 576], P('dp', 'seq')
- weight_grad: float32 [512, 16384], P(None, 'seq')
The draws below stay inside these ranges and needn't reach their ends.
All inputs are finite; a program needn't handle non-finite values.
Results may differ from the reference program's by a relative error of at most 0.023.
Values may be sent and summed in bfloat16 or wider, within the bound.
No kernel may reach another device: no remote copies, remote signals or barrier semaphores. Data moves between devices by JAX's collectives and lax.ppermute only.
A program may use at most 192 MiB of HBM per device.

```python
import jax
import jax.numpy as jnp
from jax import lax

HEADS = 64
NOPE = 128
ROPE = 64
VDIM = 128
LATENT = 512
SEQLEN = 1024
SLABS = 16


def draw_queries(key, part):
    key = jax.random.fold_in(key, 5)
    shape = (SLABS, SEQLEN, HEADS, NOPE + ROPE)
    values = jnp.clip(jax.random.normal(key, shape, jnp.float32), -6.0, 6.0)
    return values.reshape(SLABS, SEQLEN, HEADS * (NOPE + ROPE)).astype(jnp.bfloat16)


def draw_latents(key, part):
    key = jax.random.fold_in(key, 8)
    shape = (SLABS, SEQLEN, LATENT + ROPE)
    values = jnp.clip(jax.random.normal(key, shape, jnp.float32), -6.0, 6.0)
    return values.astype(jnp.bfloat16)


def levels(key, dims, cuts, least, top_value):
    factor_of, own = 1.0, jax.random.fold_in(key, 6)
    for axis_at, blocks in cuts:
        draws = jnp.exp(jax.random.uniform(jax.random.fold_in(own, axis_at), (blocks,), jnp.float32, least / len(cuts), top_value / len(cuts)))
        factor_of = factor_of * jnp.repeat(draws, dims[axis_at] // blocks).reshape([-1 if axis == axis_at else 1 for axis in range(len(dims))])
    return factor_of


def scatter_about(stream_key, extent, scale, limit, cuts=(), kind=jnp.bfloat16):
    values = jax.random.normal(stream_key, extent, jnp.float32) * scale
    if len(cuts) > 0:
        values = levels(stream_key, extent, cuts, -0.22, 0.18) * values
    return jnp.clip(values, min=-limit, max=limit).astype(kind)


def setup_inputs(seed: int = 0) -> dict:
    seeds = jax.random.split(jax.random.key(seed), 5)
    queries = draw_queries(jax.random.fold_in(seeds[4], 71), 0)
    latents = draw_latents(jax.random.fold_in(seeds[4], 71), 0)
    kv_weight = scatter_about(seeds[2], (LATENT, HEADS * (NOPE + VDIM)), LATENT ** -0.5, 0.25, ((1, 8),))
    out_grad = scatter_about(seeds[3], (SLABS, SEQLEN, HEADS * VDIM), 1.0, 6.0, ((0, 16), (1, 8)))
    return dict(queries=queries, latents=latents, kv_weight=kv_weight, out_grad=out_grad)


def slab_grads(query, latent, weight, grad):
    length = query.shape[0]
    width = NOPE + ROPE
    scale = width ** -0.5
    plain = latent[:, :LATENT]
    key_rope = latent[:, LATENT:]
    keyval = jnp.dot(plain, weight, preferred_element_type=jnp.float32).astype(jnp.bfloat16)
    keyval = keyval.reshape(length, HEADS, NOPE + VDIM)
    row_pos = lax.broadcasted_iota(jnp.int32, (length, length), 0)
    col_pos = lax.broadcasted_iota(jnp.int32, (length, length), 1)
    allowed = col_pos <= row_pos

    def one_head(items):
        q_head, kv_head, g_head = items
        key_full = jnp.concatenate([kv_head[:, :NOPE], key_rope], axis=1)
        value = kv_head[:, NOPE:]
        scores = jnp.dot(q_head, key_full.T, preferred_element_type=jnp.float32) * scale
        scores = jnp.where(allowed, scores, -jnp.inf)
        top = jnp.max(scores, axis=1, keepdims=True)
        expo = jnp.exp(scores - top)
        probs = expo / jnp.sum(expo, axis=1, keepdims=True)
        probs_low = probs.astype(jnp.bfloat16)
        attended = jnp.dot(probs_low, value, preferred_element_type=jnp.float32)
        delta = jnp.sum(g_head.astype(jnp.float32) * attended, axis=1, keepdims=True)
        dprobs = jnp.dot(g_head, value.T, preferred_element_type=jnp.float32)
        dscores = (probs * (dprobs - delta)).astype(jnp.bfloat16)
        dquery = jnp.dot(dscores, key_full, preferred_element_type=jnp.float32) * scale
        dkey = jnp.dot(dscores.T, q_head, preferred_element_type=jnp.float32) * scale
        dvalue = jnp.dot(probs_low.T, g_head, preferred_element_type=jnp.float32)
        dkeyval = jnp.concatenate([dkey[:, :NOPE], dvalue], axis=1).astype(jnp.bfloat16)
        return dquery.astype(jnp.bfloat16), dkeyval, dkey[:, NOPE:]

    stacked = (query.reshape(length, HEADS, width).transpose(1, 0, 2),
               keyval.transpose(1, 0, 2),
               grad.reshape(length, HEADS, VDIM).transpose(1, 0, 2))
    dquery, dkeyval, drope = lax.map(one_head, stacked)
    query_grad = dquery.transpose(1, 0, 2).reshape(length, HEADS * width)
    dkv_flat = dkeyval.transpose(1, 0, 2).reshape(length, HEADS * (NOPE + VDIM))
    back = jnp.dot(dkv_flat, weight.T, preferred_element_type=jnp.float32)
    latent_grad = jnp.concatenate([back, jnp.sum(drope, axis=0)], axis=1).astype(jnp.bfloat16)
    weight_part = jnp.dot(plain.T, dkv_flat, preferred_element_type=jnp.float32)
    return query_grad, latent_grad, weight_part


def reference(queries, latents, kv_weight, out_grad):
    def step(total, items):
        query, latent, grad = items
        query_grad, latent_grad, weight_part = slab_grads(query, latent, kv_weight, grad)
        return total + weight_part, (query_grad, latent_grad)

    start = jnp.zeros((LATENT, HEADS * (NOPE + VDIM)), jnp.float32)
    total, outs = lax.scan(step, start, (queries, latents, out_grad))
    return outs[0], outs[1], total / SLABS
```

```python
import functools

import jax
import jax.numpy as jnp
from jax import lax
from jax.experimental import pallas as pl
from jax.experimental.pallas import tpu as pltpu
from jax.sharding import PartitionSpec as P

NOPE = 128
ROPE = 64
VDIM = 128
LATENT = 512
QPAIR = 2 * (NOPE + ROPE)
GPAIR = 2 * VDIM
PAIR = QPAIR + GPAIR
KVPAIR = 2 * (NOPE + VDIM)
LATPAD = 640
LOG2E = 1.4426950408889634
VMEM = 56 * 1024 * 1024
EARLY = 2
LINE = 4


def dot(a, b, dims):
    return lax.dot_general(a, b, (dims, ((), ())), preferred_element_type=jnp.float32)


def pack_kernel(plans, with_latents, *refs):
    refs = list(refs)
    q_ref, g_ref = refs[:2]
    lat_ref = refs[2] if with_latents else None
    outs = refs[2 + with_latents : 2 + with_latents + len(plans)]
    sems = refs[-1]
    groups = outs[0].shape[0]
    per_group = q_ref.shape[1] // (groups * QPAIR)
    copies = []
    for (first, pairs), out in zip(plans, outs, strict=True):
        for j in range(groups):
            for pair in range(pairs):
                at = j * per_group + first + pair
                base = pair * PAIR
                for ref, width, to in ((q_ref, QPAIR, base), (g_ref, GPAIR, base + QPAIR)):
                    copies.append(
                        pltpu.make_async_copy(
                            ref.at[:, at * width : (at + 1) * width],
                            out.at[j, :, to : to + width],
                            sems.at[len(copies)],
                        )
                    )
    for copy in copies:
        copy.start()
    if with_latents:
        base = plans[0][1] * PAIR
        rows = lat_ref[...].T
        pad = jnp.zeros((rows.shape[0], LATPAD - rows.shape[1]), rows.dtype)
        rows = jnp.concatenate([rows, pad], axis=1)
        for j in range(groups):
            outs[0][j, :, base:] = rows
    for copy in copies:
        copy.wait()


def pack(q, g, latents, groups, plans):
    tokens = q.shape[0]
    has = latents is not None
    hbm = pl.BlockSpec(memory_space=pl.ANY)
    vmem = pl.BlockSpec(memory_space=pltpu.VMEM)
    shapes = []
    for index, (_, pairs) in enumerate(plans):
        width = pairs * PAIR + (LATPAD if has and index == 0 else 0)
        shapes.append(jax.ShapeDtypeStruct((groups, tokens, width), q.dtype))
    count = sum(2 * groups * pairs for _, pairs in plans)
    return pl.pallas_call(
        functools.partial(pack_kernel, plans, has),
        in_specs=[hbm, hbm] + [vmem] * has,
        out_specs=[vmem] * len(plans),
        out_shape=shapes,
        scratch_shapes=[pltpu.SemaphoreType.DMA((count,))],
        compiler_params=pltpu.CompilerParams(vmem_limit_bytes=VMEM),
        cost_estimate=pl.CostEstimate(
            flops=0, bytes_accessed=sum(4 * s.size for s in shapes), transcendentals=0
        ),
        name="pack",
    )(*([q, g] + [latents] * has))


def unpack_kernel(first, pairs, has_total, with_latents, *refs):
    refs = list(refs)
    if has_total:
        refs.pop(0)
    part_ref, out_ref = refs[:2]
    groups = part_ref.shape[0]
    per_group = out_ref.shape[1] // (groups * QPAIR)
    width = pairs * QPAIR
    sems, held = refs[-2:]
    fetches, copies = [], []
    for j in range(groups):
        at = (j * per_group + first) * QPAIR
        fetches.append(pltpu.make_async_copy(part_ref.at[j], held.at[j], sems.at[0, j]))
        copies.append(
            pltpu.make_async_copy(
                held.at[j, :, :width], out_ref.at[:, at : at + width], sems.at[1, j]
            )
        )
    for fetch in fetches:
        fetch.start()
    for fetch, copy in zip(fetches, copies, strict=True):
        fetch.wait()
        copy.start()
    if with_latents:
        total = held[0, :, width:].astype(jnp.float32)
        for j in range(1, groups):
            total += held[j, :, width:].astype(jnp.float32)
        refs[2][...] = total.T[: LATENT + ROPE].astype(part_ref.dtype)
    for copy in copies:
        copy.wait()


def unpack(total, part, first, pairs, per_group, with_latents):
    groups, tokens, _ = part.shape
    hbm = pl.BlockSpec(memory_space=pl.ANY)
    out_specs = [hbm]
    shapes = [jax.ShapeDtypeStruct((tokens, groups * per_group * QPAIR), part.dtype)]
    if with_latents:
        out_specs.append(pl.BlockSpec(memory_space=pltpu.VMEM))
        shapes.append(jax.ShapeDtypeStruct((LATENT + ROPE, tokens), part.dtype))
    has = total is not None
    return pl.pallas_call(
        functools.partial(unpack_kernel, first, pairs, has, with_latents),
        in_specs=[hbm] * (1 + has),
        out_specs=out_specs,
        out_shape=shapes,
        scratch_shapes=[
            pltpu.SemaphoreType.DMA((2, groups)),
            pltpu.VMEM(part.shape, part.dtype),
        ],
        input_output_aliases={0: 0} if has else {},
        compiler_params=pltpu.CompilerParams(vmem_limit_bytes=VMEM),
        cost_estimate=pl.CostEstimate(
            flops=0, bytes_accessed=4 * groups * tokens * pairs * QPAIR, transcendentals=0
        ),
        name="unpack",
    )(*([total] * has + [part]))


def one_head(q_ref, q_at, g_ref, g_at, key, value, dk_ref, dv_ref, scale, block):
    span = key.shape[0]
    dq_rows = []
    for index in reversed(range(span // block)):
        first, limit = index * block, (index + 1) * block
        q = q_ref[first:limit, q_at : q_at + 256]
        g = g_ref[first:limit, g_at : g_at + VDIM]
        keys, values = key[:limit], value[:limit]
        scores = dot(keys, q, ((1,), (1,)))
        key_pos = lax.broadcasted_iota(jnp.int32, (block, block), 0)
        query_pos = lax.broadcasted_iota(jnp.int32, (block, block), 1)
        last = jnp.where(key_pos <= query_pos, scores[first:], -jnp.inf)
        scores = jnp.concatenate([scores[:first], last], axis=0) if index else last
        top = jnp.max(scores, axis=0, keepdims=True)
        expo = jnp.exp2((scores - top) * (scale * LOG2E))
        probs = expo * (1.0 / jnp.sum(expo, axis=0, keepdims=True))
        dprobs = dot(values, g, ((1,), (1,)))
        delta = jnp.sum(probs * dprobs, axis=0, keepdims=True)
        dscores = (probs * (dprobs - delta)).astype(jnp.bfloat16)
        dv = dot(probs.astype(jnp.bfloat16), g, ((1,), (0,)))
        dk = dot(dscores, q, ((1,), (0,)))
        if limit == span:
            dv_ref[...] = dv
            dk_ref[...] = dk
        else:
            dv_ref[:limit] += dv
            dk_ref[:limit] += dk
        dq_rows.append(dot(dscores, keys, ((0,), (0,))))
    return jnp.concatenate(dq_rows[::-1], axis=0)


def attend_kernel(has_sum, last, *refs):
    refs = list(refs)
    place, lat_ref, w_ref, x_ref = refs[:4]
    rest = refs[4:]
    sum_in = rest.pop(0) if has_sum else None
    if has_sum and not last:
        rest = rest[3:]
    if last:
        dq_ref, keep_ref, send_ref, total, dk0, dv0, dk1, dv1 = rest
    else:
        dq_ref, keep_ref, send_ref, out_ref, total, dk0, dv0, dk1, dv1 = rest
    step = pl.program_id(0)
    scale = (NOPE + ROPE) ** (-0.5)
    half = NOPE // 2
    span = lat_ref.shape[0]
    block = min(256, span)
    plain = lat_ref[:, :LATENT]
    rope = lat_ref[:, LATENT:]
    keyval = dot(plain, w_ref[...], ((1,), (0,)))
    lane = lax.broadcasted_iota(jnp.int32, (span, NOPE), 1)
    key0 = jnp.concatenate([keyval[:, :NOPE].astype(jnp.bfloat16), rope], axis=1)
    value0 = keyval[:, NOPE : 2 * NOPE].astype(jnp.bfloat16)
    moved = pltpu.roll(keyval[:, 2 * NOPE : 3 * NOPE], half, 1)
    rope_moved = pltpu.roll(rope.astype(jnp.float32), half, 1)
    key1 = jnp.concatenate(
        [jnp.where(lane < half, 0.0, moved), jnp.where(lane < half, moved, rope_moved)], axis=1
    ).astype(jnp.bfloat16)
    value1 = keyval[:, 3 * NOPE :].astype(jnp.bfloat16)
    q_ref, g_at = x_ref, QPAIR
    dq0 = one_head(q_ref, 0, x_ref, g_at, key0, value0, dk0, dv0, scale, block)
    dq1 = one_head(q_ref, NOPE, x_ref, g_at + VDIM, key1, value1, dk1, dv1, scale, block)
    dq = jnp.concatenate([dq0[:, :NOPE], dq0[:, NOPE:] + dq1[:, :NOPE], dq1[:, NOPE:]], axis=1)
    dq = (dq * scale).astype(jnp.bfloat16)
    if last:
        dq_ref[:, pl.ds(pl.multiple_of(step * QPAIR, QPAIR), QPAIR)] = dq
    else:
        dq_ref[...] = dq
    left = pltpu.roll(dk1[:, :NOPE], half, 1)
    right = pltpu.roll(dk1[:, NOPE:], half, 1)
    dkeyval = jnp.concatenate(
        [
            dk0[:, :NOPE] * scale,
            dv0[...],
            jnp.where(lane < half, left, right) * scale,
            dv1[...],
        ],
        axis=1,
    ).astype(jnp.bfloat16)
    drope = jnp.where(lane < half, (dk0[:, NOPE:] + right) * scale, 0.0)
    back = dot(dkeyval, w_ref[...], ((1,), (1,)))
    dw = dot(plain, dkeyval, ((0,), (0,))).astype(jnp.bfloat16)
    rows = LATENT // 2 // LINE
    for at in range(2 * LINE):
        to = lax.rem(at % LINE - place[1] + LINE, LINE)
        to = pl.ds(pl.multiple_of(to * rows, rows), rows)
        piece = dw[at * rows : (at + 1) * rows]

        @pl.when(place[0] == at // LINE)
        def _():
            keep_ref[to, :] = piece

        @pl.when(place[0] != at // LINE)
        def _():
            send_ref[to, :] = piece

    @pl.when(step == 0)
    def _():
        if has_sum:
            total[:, :LATENT] = back + sum_in[:, :LATENT]
            total[:, LATENT:] = drope + sum_in[:, LATENT:]
        else:
            total[:, :LATENT] = back
            total[:, LATENT:] = drope

    @pl.when(step > 0)
    def _():
        total[:, :LATENT] += back
        total[:, LATENT:] += drope

    @pl.when(step == pl.num_programs(0) - 1)
    def _():
        if last:
            dq_ref[:, dq_ref.shape[1] - LATPAD :] = total[...].astype(jnp.bfloat16)
        else:
            out_ref[...] = total[...]


def attend(place, lat, lat_block, weight, first, x, pairs, held, last):
    span = lat.shape[0]
    f32, bf16 = jnp.float32, jnp.bfloat16
    whole = lambda j: (0, 0)
    hbm = pl.BlockSpec(memory_space=pl.ANY)
    specs = [
        pl.BlockSpec(memory_space=pltpu.SMEM),
        pl.BlockSpec((span, LATPAD), lambda j: (0, lat_block)),
        pl.BlockSpec((LATENT, KVPAIR), lambda j: (0, first + j)),
        pl.BlockSpec((span, PAIR), lambda j: (0, j)),
    ]
    args = [place, lat, weight, x]
    aliases = {}
    if held is not None:
        specs.append(pl.BlockSpec((span, LATPAD), whole))
        args.append(held[3])
    start = 0 if last else first
    dw_specs = [pl.BlockSpec((LATENT // 2, KVPAIR), lambda j: (0, start + j))] * 2
    dw_shapes = [jax.ShapeDtypeStruct((LATENT // 2, (pairs if last else EARLY) * KVPAIR), bf16)] * 2
    if last:
        width = pairs * QPAIR + LATPAD
        out_specs = [pl.BlockSpec((span, width), whole)] + dw_specs
        shapes = [jax.ShapeDtypeStruct((span, width), bf16)] + dw_shapes
    else:
        out_specs = [pl.BlockSpec((span, QPAIR), lambda j: (0, first + j))] + dw_specs
        out_specs.append(pl.BlockSpec((span, LATPAD), whole))
        shapes = [jax.ShapeDtypeStruct((span, EARLY * QPAIR), bf16)] + dw_shapes
        shapes.append(jax.ShapeDtypeStruct((span, LATPAD), f32))
        if held is not None:
            aliases = {5: 0, 6: 1, 7: 2}
            specs += [hbm] * 3
            args += held[:3]
    return pl.pallas_call(
        functools.partial(attend_kernel, held is not None, last),
        grid=(pairs,),
        in_specs=specs,
        out_specs=out_specs,
        out_shape=shapes,
        input_output_aliases=aliases,
        scratch_shapes=[
            pltpu.VMEM((span, LATPAD), f32),
            pltpu.VMEM((span, 2 * NOPE), f32),
            pltpu.VMEM((span, VDIM), f32),
            pltpu.VMEM((span, 2 * NOPE), f32),
            pltpu.VMEM((span, VDIM), f32),
        ],
        compiler_params=pltpu.CompilerParams(vmem_limit_bytes=VMEM),
        cost_estimate=pl.CostEstimate(
            flops=pairs * 5_000_000_000, bytes_accessed=pairs * 6_000_000, transcendentals=0
        ),
        name="attend",
    )(*args)


def exchange(x, axis, groups=None):
    return lax.all_to_all(x, axis, split_axis=0, concat_axis=0, tiled=True, axis_index_groups=groups)


def send(x, step):
    slabs = lax.axis_size("dp")
    return lax.ppermute(x, "dp", [(i, step(i)) for i in range(slabs)])


def along(step):
    def to(i):
        near = 2 * LINE
        return i // near * near + ((i // 2 + step) % LINE) * 2 + i % 2

    return to


def add_kernel(*refs):
    *parts, out_ref = refs
    total = parts[0][...].astype(jnp.float32)
    for part in parts[1:]:
        total += part[...].astype(jnp.float32)
    out_ref[...] = total.astype(out_ref.dtype)


def add(*parts):
    return pl.pallas_call(add_kernel, out_shape=parts[0], name="add")(*parts)


def split_kernel(keep_ref, got_ref, *out_refs):
    total = keep_ref[...].astype(jnp.float32) + got_ref[...].astype(jnp.float32)
    rows = out_refs[0].shape[0]
    for index, out_ref in enumerate(out_refs):
        out_ref[...] = total[index * rows : (index + 1) * rows].astype(out_ref.dtype)


def split(keep, got):
    shape = jax.ShapeDtypeStruct((keep.shape[0] // LINE, keep.shape[1]), keep.dtype)
    return pl.pallas_call(split_kernel, out_shape=[shape] * LINE, name="split")(keep, got)


def scatter_slabs(keep, give):
    own, *others = split(keep, send(give, lambda i: i ^ 1))
    part = add(own, *[send(x, along(k + 1)) for k, x in enumerate(others)])
    near = 2 * LINE
    return add(part, send(part, lambda i: (i + near) % (2 * near)))


def gather_slabs(part):
    mine = jnp.concatenate([part] + [send(part, along(k)) for k in range(1, LINE)], axis=0)
    return mine, send(mine, lambda i: i ^ 1)


def place_kernel(slabs, place, *refs):
    *parts, out_ref = refs
    rows = parts[0].shape[0] // LINE
    column = 0
    for mine, other in zip(parts[::2], parts[1::2], strict=True):
        width = mine.shape[1]
        for ref, core in ((mine, place[0]), (other, 1 - place[0])):
            for k in range(LINE):
                at = core * LINE + lax.rem(place[1] - k + LINE, LINE)
                to = pl.ds(pl.multiple_of(at * rows, rows), rows)
                piece = ref[k * rows : (k + 1) * rows].astype(jnp.float32)
                out_ref[to, column : column + width] = piece * (1.0 / slabs)
        column += width


def place_slabs(place, *parts):
    width = sum(part.shape[1] for part in parts) // 2
    vmem = pl.BlockSpec(memory_space=pltpu.VMEM)
    return pl.pallas_call(
        functools.partial(place_kernel, lax.axis_size("dp")),
        in_specs=[pl.BlockSpec(memory_space=pltpu.SMEM)] + [vmem] * len(parts),
        out_specs=vmem,
        out_shape=jax.ShapeDtypeStruct((LATENT, width), jnp.float32),
        compiler_params=pltpu.CompilerParams(vmem_limit_bytes=VMEM),
        name="place",
    )(place, *parts)


def after(x, *others):
    return lax.optimization_barrier((x,) + others)


def shards(queries, latents, kv_weight, out_grad):
    groups = lax.axis_size("seq")
    tokens = queries.shape[1]
    span = tokens * groups
    per_group = kv_weight.shape[1] // KVPAIR
    late = per_group - EARLY
    q, g, lat = queries[0], out_grad[0], latents[0].T
    me = lax.axis_index("dp")
    place = jnp.stack([me % 2, me // 2 % LINE]).astype(jnp.int32)

    (x0,) = pack(q, g, lat, groups, ((0, 1),))
    x1, x2 = pack(q, g, None, groups, ((1, 1), (2, late)))
    got0 = exchange(x0, "seq")
    x1, got0 = after(x1, got0)
    got1 = exchange(x1, "seq")
    got0 = got0.reshape(span, got0.shape[2])
    held = attend(place, got0, 1, kv_weight, 0, got0, 1, None, False)
    x2, got1, *held = after(x2, got1, *held)
    got2 = exchange(x2, "seq")
    dq, keep0, give0, total = attend(
        place, got0, 1, kv_weight, 1, got1.reshape(span, PAIR), 1, held, False
    )
    back0 = exchange(dq.reshape(groups, tokens, EARLY * QPAIR), "seq")
    part0 = scatter_slabs(keep0, give0)
    total, part0 = after(total, part0)
    send1, keep1, give1 = attend(
        place, got0, 1, kv_weight, 2, got2.reshape(span, late * PAIR), late, (0, 0, 0, total), True
    )
    keep1, give1, part0, back0 = after(keep1, give1, part0, back0)
    back1 = exchange(send1.reshape(groups, tokens, send1.shape[1]), "seq")
    part1 = scatter_slabs(keep1, give1)
    (query_grad,) = unpack(None, back0, 0, EARLY, per_group, False)
    weight_grad = place_slabs(place, *gather_slabs(part0), *gather_slabs(part1))
    query_grad, latent_grad = unpack(query_grad, back1, EARLY, late, per_group, True)
    return (query_grad[None], latent_grad.T[None], weight_grad)


def solution(mesh):
    placed = (P("dp", "seq", None), P("dp", "seq", None), P(None, "seq"), P("dp", "seq", None))
    return jax.shard_map(
        shards,
        mesh=mesh,
        in_specs=placed,
        out_specs=(P("dp", "seq", None), P("dp", "seq", None), P(None, "seq")),
        check_vma=False,
    )
```

```python
import functools

import jax
import jax.numpy as jnp
from jax import lax
from jax.experimental import pallas as pl
from jax.experimental.pallas import tpu as pltpu
from jax.sharding import PartitionSpec as P

NOPE = 128
ROPE = 64
VDIM = 128
LATENT = 512
QPAIR = 2 * (NOPE + ROPE)
GPAIR = 2 * VDIM
PAIR = QPAIR + GPAIR
KVPAIR = 2 * (NOPE + VDIM)
LATPAD = 640
LOG2E = 1.4426950408889634
VMEM = 56 * 1024 * 1024
EARLY = 2
LINE = 4


def dot(a, b, dims):
    return lax.dot_general(a, b, (dims, ((), ())), preferred_element_type=jnp.float32)


def pack_kernel(plans, q_ref, g_ref, lat_ref, *refs):
    count = len(plans)
    outs, held, sems, sent = refs[:count], refs[count : 2 * count], refs[-2], refs[-1]
    groups = outs[0].shape[0]
    per_group = q_ref.shape[1] // (groups * QPAIR)
    batches, number = [], 0
    for n, (first, pairs) in enumerate(plans):
        for j in range(groups):
            batch = []
            at = j * per_group + first
            for ref, width, to in ((q_ref, QPAIR, 0), (g_ref, GPAIR, pairs * QPAIR)):
                batch.append(
                    pltpu.make_async_copy(
                        ref.at[:, at * width : (at + pairs) * width],
                        held[n].at[j, :, to : to + pairs * width],
                        sems.at[number],
                    )
                )
                number += 1
            leave = pltpu.make_async_copy(held[n].at[j], outs[n].at[j], sent.at[n, j])
            batches.append((batch, leave))
    for batch, _ in batches:
        for copy in batch:
            copy.start()
    base = plans[0][1] * PAIR
    rows = lat_ref[...].T
    pad = jnp.zeros((rows.shape[0], LATPAD - rows.shape[1]), rows.dtype)
    rows = jnp.concatenate([rows, pad], axis=1)
    for j in range(groups):
        held[0][j, :, base:] = rows
    for batch, leave in batches:
        for copy in batch:
            copy.wait()
        leave.start()
    for _, leave in batches:
        leave.wait()


def pack(q, g, latents, groups, plans):
    tokens = q.shape[0]
    hbm = pl.BlockSpec(memory_space=pl.ANY)
    shapes = []
    for index, (_, pairs) in enumerate(plans):
        width = pairs * PAIR + (LATPAD if index == 0 else 0)
        shapes.append(jax.ShapeDtypeStruct((groups, tokens, width), q.dtype))
    return pl.pallas_call(
        functools.partial(pack_kernel, plans),
        in_specs=[hbm, hbm, pl.BlockSpec(memory_space=pltpu.VMEM)],
        out_specs=[hbm] * len(plans),
        out_shape=shapes,
        scratch_shapes=[pltpu.VMEM(shape.shape, shape.dtype) for shape in shapes]
        + [
            pltpu.SemaphoreType.DMA((2 * groups * len(plans),)),
            pltpu.SemaphoreType.DMA((len(plans), groups)),
        ],
        compiler_params=pltpu.CompilerParams(vmem_limit_bytes=VMEM),
        cost_estimate=pl.CostEstimate(
            flops=0, bytes_accessed=sum(4 * s.size for s in shapes), transcendentals=0
        ),
        name="pack",
    )(q, g, latents)


def unpack_kernel(plans, *refs):
    count = len(plans)
    parts, out_ref, sems = refs[:count], refs[count], refs[count + 1]
    helds = refs[count + 2 :]
    groups = parts[0].shape[0]
    per_group = out_ref.shape[1] // (groups * QPAIR)
    fetches, copies = [], []
    for n, (first, pairs) in enumerate(plans):
        width = pairs * QPAIR
        for j in range(groups):
            at = (j * per_group + first) * QPAIR
            fetches.append(
                pltpu.make_async_copy(parts[n].at[j], helds[n].at[j], sems.at[0, n, j])
            )
            copies.append(
                pltpu.make_async_copy(
                    helds[n].at[j], out_ref.at[:, at : at + width], sems.at[1, n, j]
                )
            )
    for fetch in fetches:
        fetch.start()
    for fetch, copy in zip(fetches, copies, strict=True):
        fetch.wait()
        copy.start()
    for copy in copies:
        copy.wait()


def unpack(parts, plans, per_group):
    groups, tokens, _ = parts[0].shape
    hbm = pl.BlockSpec(memory_space=pl.ANY)
    size = tokens * groups * per_group * QPAIR
    return pl.pallas_call(
        functools.partial(unpack_kernel, plans),
        in_specs=[hbm] * len(parts),
        out_specs=hbm,
        out_shape=jax.ShapeDtypeStruct((tokens, groups * per_group * QPAIR), parts[0].dtype),
        scratch_shapes=[pltpu.SemaphoreType.DMA((2, len(parts), groups))]
        + [pltpu.VMEM(part.shape, part.dtype) for part in parts],
        compiler_params=pltpu.CompilerParams(vmem_limit_bytes=VMEM),
        cost_estimate=pl.CostEstimate(flops=0, bytes_accessed=4 * size, transcendentals=0),
        name="unpack",
    )(*parts)


def collect_kernel(part_ref, out_ref):
    total = part_ref[0].astype(jnp.float32)
    for j in range(1, part_ref.shape[0]):
        total += part_ref[j].astype(jnp.float32)
    out_ref[...] = total.T[: LATENT + ROPE].astype(out_ref.dtype)


def collect(part):
    shape = jax.ShapeDtypeStruct((LATENT + ROPE, part.shape[1]), part.dtype)
    return pl.pallas_call(collect_kernel, out_shape=shape, name="collect")(part)


def one_head(q_ref, q_at, g_ref, g_at, key, value, dk_ref, dv_ref, scale, block):
    span = key.shape[0]
    dq_rows = []
    for index in reversed(range(span // block)):
        first, limit = index * block, (index + 1) * block
        q = q_ref[first:limit, q_at : q_at + 256]
        g = g_ref[first:limit, g_at : g_at + VDIM]
        keys, values = key[:limit], value[:limit]
        scores = dot(keys, q, ((1,), (1,)))
        key_pos = lax.broadcasted_iota(jnp.int32, (block, block), 0)
        query_pos = lax.broadcasted_iota(jnp.int32, (block, block), 1)
        last = jnp.where(key_pos <= query_pos, scores[first:], -jnp.inf)
        scores = jnp.concatenate([scores[:first], last], axis=0) if index else last
        top = jnp.max(scores, axis=0, keepdims=True)
        expo = jnp.exp2((scores - top) * (scale * LOG2E))
        probs = expo * (1.0 / jnp.sum(expo, axis=0, keepdims=True))
        dprobs = dot(values, g, ((1,), (1,)))
        delta = jnp.sum(probs * dprobs, axis=0, keepdims=True)
        dscores = (probs * (dprobs - delta)).astype(jnp.bfloat16)
        dv = dot(probs.astype(jnp.bfloat16), g, ((1,), (0,)))
        dk = dot(dscores, q, ((1,), (0,)))
        if limit == span:
            dv_ref[...] = dv
            dk_ref[...] = dk
        else:
            dv_ref[:limit] += dv
            dk_ref[:limit] += dk
        dq_rows.append(dot(dscores, keys, ((0,), (0,))))
    return jnp.concatenate(dq_rows[::-1], axis=0)


def attend_kernel(has_sum, *refs):
    refs = list(refs)
    place, lat_ref, w_ref, q_ref, g_ref = refs[:5]
    rest = refs[5:]
    sum_in = rest.pop(0) if has_sum else None
    dq_ref, keep_ref, send_ref, out_ref, total, dk0, dv0, dk1, dv1 = rest
    step = pl.program_id(0)
    scale = (NOPE + ROPE) ** (-0.5)
    half = NOPE // 2
    span = lat_ref.shape[0]
    block = min(256, span)
    plain = lat_ref[:, :LATENT]
    rope = lat_ref[:, LATENT:]
    keyval = dot(plain, w_ref[...], ((1,), (0,)))
    lane = lax.broadcasted_iota(jnp.int32, (span, NOPE), 1)
    key0 = jnp.concatenate([keyval[:, :NOPE].astype(jnp.bfloat16), rope], axis=1)
    value0 = keyval[:, NOPE : 2 * NOPE].astype(jnp.bfloat16)
    moved = pltpu.roll(keyval[:, 2 * NOPE : 3 * NOPE], half, 1)
    rope_moved = pltpu.roll(rope.astype(jnp.float32), half, 1)
    key1 = jnp.concatenate(
        [jnp.where(lane < half, 0.0, moved), jnp.where(lane < half, moved, rope_moved)], axis=1
    ).astype(jnp.bfloat16)
    value1 = keyval[:, 3 * NOPE :].astype(jnp.bfloat16)
    dq0 = one_head(q_ref, 0, g_ref, 0, key0, value0, dk0, dv0, scale, block)
    dq1 = one_head(q_ref, NOPE, g_ref, VDIM, key1, value1, dk1, dv1, scale, block)
    dq = jnp.concatenate([dq0[:, :NOPE], dq0[:, NOPE:] + dq1[:, :NOPE], dq1[:, NOPE:]], axis=1)
    dq = (dq * scale).astype(jnp.bfloat16)
    dq_ref[...] = dq
    left = pltpu.roll(dk1[:, :NOPE], half, 1)
    right = pltpu.roll(dk1[:, NOPE:], half, 1)
    dkeyval = jnp.concatenate(
        [
            dk0[:, :NOPE] * scale,
            dv0[...],
            jnp.where(lane < half, left, right) * scale,
            dv1[...],
        ],
        axis=1,
    ).astype(jnp.bfloat16)
    drope = jnp.where(lane < half, (dk0[:, NOPE:] + right) * scale, 0.0)
    back = dot(dkeyval, w_ref[...], ((1,), (1,)))
    dw = dot(plain, dkeyval, ((0,), (0,))).astype(jnp.bfloat16)
    rows = LATENT // 2 // LINE
    for at in range(2 * LINE):
        to = lax.rem(at % LINE - place[1] + LINE, LINE)
        to = pl.ds(pl.multiple_of(to * rows, rows), rows)
        piece = dw[at * rows : (at + 1) * rows]

        @pl.when(place[0] == at // LINE)
        def _():
            keep_ref[to, :] = piece

        @pl.when(place[0] != at // LINE)
        def _():
            send_ref[to, :] = piece

    @pl.when(step == 0)
    def _():
        if has_sum:
            total[:, :LATENT] = back + sum_in[:, :LATENT]
            total[:, LATENT:] = drope + sum_in[:, LATENT:]
        else:
            total[:, :LATENT] = back
            total[:, LATENT:] = drope

    @pl.when(step > 0)
    def _():
        total[:, :LATENT] += back
        total[:, LATENT:] += drope

    @pl.when(step == pl.num_programs(0) - 1)
    def _():
        out_ref[...] = total[...].astype(out_ref.dtype)


def attend(place, lat, lat_block, weight, first, x, pairs, total, total_type):
    span = lat.shape[0]
    f32, bf16 = jnp.float32, jnp.bfloat16
    whole = lambda j: (0, 0)
    column = lambda j: (0, j)
    specs = [
        pl.BlockSpec(memory_space=pltpu.SMEM),
        pl.BlockSpec((span, LATPAD), lambda j: (0, lat_block)),
        pl.BlockSpec((LATENT, KVPAIR), lambda j: (0, first + j)),
        pl.BlockSpec((span, QPAIR), column),
        pl.BlockSpec((span, GPAIR), lambda j: (0, pairs * QPAIR // GPAIR + j)),
    ]
    args = [place, lat, weight, x, x]
    if total is not None:
        specs.append(pl.BlockSpec((span, LATPAD), whole))
        args.append(total)
    dw_shape = jax.ShapeDtypeStruct((LATENT // 2, pairs * KVPAIR), bf16)
    return pl.pallas_call(
        functools.partial(attend_kernel, total is not None),
        grid=(pairs,),
        in_specs=specs,
        out_specs=[
            pl.BlockSpec((span, QPAIR), column),
            pl.BlockSpec((LATENT // 2, KVPAIR), column),
            pl.BlockSpec((LATENT // 2, KVPAIR), column),
            pl.BlockSpec((span, LATPAD), whole),
        ],
        out_shape=[
            jax.ShapeDtypeStruct((span, pairs * QPAIR), bf16),
            dw_shape,
            dw_shape,
            jax.ShapeDtypeStruct((span, LATPAD), total_type),
        ],
        scratch_shapes=[
            pltpu.VMEM((span, LATPAD), f32),
            pltpu.VMEM((span, 2 * NOPE), f32),
            pltpu.VMEM((span, VDIM), f32),
            pltpu.VMEM((span, 2 * NOPE), f32),
            pltpu.VMEM((span, VDIM), f32),
        ],
        compiler_params=pltpu.CompilerParams(vmem_limit_bytes=VMEM),
        cost_estimate=pl.CostEstimate(
            flops=pairs * 5_000_000_000, bytes_accessed=pairs * 6_000_000, transcendentals=0
        ),
        name="attend",
    )(*args)


def exchange(x, axis, groups=None):
    return lax.all_to_all(x, axis, split_axis=0, concat_axis=0, tiled=True, axis_index_groups=groups)


def send(x, step):
    slabs = lax.axis_size("dp")
    return lax.ppermute(x, "dp", [(i, step(i)) for i in range(slabs)])


def along(step):
    def to(i):
        near = 2 * LINE
        return i // near * near + ((i // 2 + step) % LINE) * 2 + i % 2

    return to


def add_kernel(*refs):
    *parts, out_ref = refs
    total = parts[0][...].astype(jnp.float32)
    for part in parts[1:]:
        total += part[...].astype(jnp.float32)
    out_ref[...] = total.astype(out_ref.dtype)


def add(*parts):
    return pl.pallas_call(add_kernel, out_shape=parts[0], name="add")(*parts)


def split_kernel(keep_ref, got_ref, *out_refs):
    total = keep_ref[...].astype(jnp.float32) + got_ref[...].astype(jnp.float32)
    rows = out_refs[0].shape[0]
    for index, out_ref in enumerate(out_refs):
        out_ref[...] = total[index * rows : (index + 1) * rows].astype(out_ref.dtype)


def split(keep, got):
    shape = jax.ShapeDtypeStruct((keep.shape[0] // LINE, keep.shape[1]), keep.dtype)
    return pl.pallas_call(split_kernel, out_shape=[shape] * LINE, name="split")(keep, got)


def swap(x):
    return send(x, lambda i: i ^ 1)


def spread(pieces):
    return [pieces[0]] + [send(x, along(k + 1)) for k, x in enumerate(pieces[1:])]


def across(part):
    slabs = 4 * LINE
    return send(part, lambda i: (i + slabs // 2) % slabs)


def gather_line(part):
    return jnp.concatenate(spread([part] * LINE), axis=0)


def place_kernel(slabs, place, *refs):
    mine, other, out_ref = refs[-3:]
    rows = mine.shape[0] // LINE
    for ref, core in ((mine, place[0]), (other, 1 - place[0])):
        for k in range(LINE):
            at = core * LINE + lax.rem(place[1] - k + LINE, LINE)
            to = pl.ds(pl.multiple_of(at * rows, rows), rows)
            out_ref[to, :] = ref[k * rows : (k + 1) * rows].astype(jnp.float32) * (1.0 / slabs)


def place_slabs(place, total, mine, other, index, count):
    whole = pl.BlockSpec(mine.shape, lambda j: (0, 0))
    has = total is not None
    return pl.pallas_call(
        functools.partial(place_kernel, lax.axis_size("dp")),
        grid=(1,),
        in_specs=[pl.BlockSpec(memory_space=pltpu.SMEM)]
        + [pl.BlockSpec(memory_space=pl.ANY)] * has
        + [whole, whole],
        out_specs=pl.BlockSpec((LATENT, mine.shape[1]), lambda j: (0, index)),
        out_shape=jax.ShapeDtypeStruct((LATENT, count * mine.shape[1]), jnp.float32),
        input_output_aliases={1: 0} if has else {},
        compiler_params=pltpu.CompilerParams(vmem_limit_bytes=VMEM),
        name="place",
    )(*([place] + [total] * has + [mine, other]))


def after(x, *others):
    return lax.optimization_barrier((x,) + others)


def shards(queries, latents, kv_weight, out_grad):
    groups = lax.axis_size("seq")
    tokens = queries.shape[1]
    span = tokens * groups
    per_group = kv_weight.shape[1] // KVPAIR
    late = per_group - EARLY
    q, g, lat = queries[0], out_grad[0], latents[0].T
    me = lax.axis_index("dp")
    place = jnp.stack([me % 2, me // 2 % LINE]).astype(jnp.int32)

    x0, x1 = pack(q, g, lat, groups, ((0, EARLY), (EARLY, late)))
    got0 = exchange(x0, "seq")
    x1, got0 = after(x1, got0)
    got1 = exchange(x1, "seq")
    lat = got0.reshape(span, got0.shape[2])
    kv = (place, lat, EARLY * PAIR // LATPAD, kv_weight)
    dq0, keep0, give0, total = attend(*kv, 0, lat, EARLY, None, jnp.float32)
    part0 = add(*spread(split(keep0, swap(give0))))
    other0 = across(part0)
    dq0, got1, part0 = after(dq0, got1, part0)
    back0 = exchange(dq0.reshape(groups, tokens, EARLY * QPAIR), "seq")
    dq1, keep1, give1, total = attend(
        *kv, EARLY, got1.reshape(span, -1), late, total, jnp.bfloat16
    )
    dq1, back0, other0 = after(dq1, back0, other0)
    back1 = exchange(dq1.reshape(groups, tokens, late * QPAIR), "seq")
    part0 = add(part0, other0)
    got, keep1, part0 = after(swap(give1), keep1, part0)
    part1 = add(*spread(split(keep1, got)))
    other1 = across(part1)
    mine0 = gather_line(part0)
    total, back1, other1, mine0 = after(total, back1, other1, mine0)
    back2 = exchange(total.reshape(groups, tokens, LATPAD), "seq")
    theirs0 = swap(mine0)
    line1 = spread([add(part1, other1)] * LINE)
    query_grad = unpack([back0, back1], ((0, EARLY), (EARLY, late)), per_group)
    weight_grad = place_slabs(place, None, mine0, theirs0, 0, 2)
    query_grad, weight_grad, *line1 = after(query_grad, weight_grad, *line1)
    mine1 = jnp.concatenate(line1, axis=0)
    weight_grad = place_slabs(place, weight_grad, mine1, swap(mine1), 1, 2)
    latent_grad = collect(back2)
    return (query_grad[None], latent_grad.T[None], weight_grad)


def solution(mesh):
    placed = (P("dp", "seq", None), P("dp", "seq", None), P(None, "seq"), P("dp", "seq", None))
    return jax.shard_map(
        shards,
        mesh=mesh,
        in_specs=placed,
        out_specs=(P("dp", "seq", None), P("dp", "seq", None), P(None, "seq")),
        check_vma=False,
    )
```

```python
import functools

import jax
import jax.numpy as jnp
from jax import lax
from jax.experimental import pallas as pl
from jax.experimental.pallas import tpu as pltpu
from jax.sharding import PartitionSpec as P

NOPE = 128
ROPE = 64
VDIM = 128
LATENT = 512
QPAIR = 2 * (NOPE + ROPE)
GPAIR = 2 * VDIM
PAIR = QPAIR + GPAIR
KVPAIR = 2 * (NOPE + VDIM)
LATPAD = 640
LOG2E = 1.4426950408889634
VMEM = 56 * 1024 * 1024
SMALL = pl.CostEstimate(flops=1, bytes_accessed=1, transcendentals=0)
EARLY = 3
LINE = 4
ADD_FLOPS = 40_000_000_000


def dot(a, b, dims):
    return lax.dot_general(a, b, (dims, ((), ())), preferred_element_type=jnp.float32)


def places(pairs):
    return (0, QPAIR) if pairs == 1 else (pairs * GPAIR, 0)


def pack_kernel(plans, q_ref, g_ref, lat_ref, *refs):
    count = len(plans)
    outs, held, sems, sent = refs[:count], refs[count : 2 * count], refs[-2], refs[-1]
    groups = outs[0].shape[0]
    per_group = q_ref.shape[1] // (groups * QPAIR)
    batches, number = [], 0
    for n, (first, pairs) in enumerate(plans):
        for j in range(groups):
            batch = []
            at = j * per_group + first
            q_at, g_at = places(pairs)
            for ref, width, to in ((q_ref, QPAIR, q_at), (g_ref, GPAIR, g_at)):
                batch.append(
                    pltpu.make_async_copy(
                        ref.at[:, at * width : (at + pairs) * width],
                        held[n].at[j, :, to : to + pairs * width],
                        sems.at[number],
                    )
                )
                number += 1
            leave = pltpu.make_async_copy(held[n].at[j], outs[n].at[j], sent.at[n, j])
            batches.append((batch, leave))
    for batch, _ in batches:
        for copy in batch:
            copy.start()
    base = plans[0][1] * PAIR
    rows = lat_ref[...].T
    pad = jnp.zeros((rows.shape[0], LATPAD - rows.shape[1]), rows.dtype)
    rows = jnp.concatenate([rows, pad], axis=1)
    for j in range(groups):
        held[0][j, :, base:] = rows
    for batch, leave in batches:
        for copy in batch:
            copy.wait()
        leave.start()
    for _, leave in batches:
        leave.wait()


def pack(q, g, latents, groups, plans):
    tokens = q.shape[0]
    hbm = pl.BlockSpec(memory_space=pl.ANY)
    shapes = []
    for index, (_, pairs) in enumerate(plans):
        width = pairs * PAIR + (LATPAD if index == 0 else 0)
        shapes.append(jax.ShapeDtypeStruct((groups, tokens, width), q.dtype))
    return pl.pallas_call(
        functools.partial(pack_kernel, plans),
        in_specs=[hbm, hbm, pl.BlockSpec(memory_space=pltpu.VMEM)],
        out_specs=[hbm] * len(plans),
        out_shape=shapes,
        scratch_shapes=[pltpu.VMEM(shape.shape, shape.dtype) for shape in shapes]
        + [
            pltpu.SemaphoreType.DMA((2 * groups * len(plans),)),
            pltpu.SemaphoreType.DMA((len(plans), groups)),
        ],
        compiler_params=pltpu.CompilerParams(vmem_limit_bytes=VMEM),
        cost_estimate=pl.CostEstimate(
            flops=0, bytes_accessed=sum(4 * s.size for s in shapes), transcendentals=0
        ),
        name="pack",
    )(q, g, latents)


def unpack_kernel(first, pairs, has_total, with_latents, *refs):
    refs = list(refs)
    if has_total:
        refs.pop(0)
    part_ref, out_ref = refs[:2]
    groups = part_ref.shape[0]
    per_group = out_ref.shape[1] // (groups * QPAIR)
    width = pairs * QPAIR
    sems, held = refs[-2:]
    fetches, copies = [], []
    for j in range(groups):
        at = (j * per_group + first) * QPAIR
        fetches.append(pltpu.make_async_copy(part_ref.at[j], held.at[j], sems.at[0, j]))
        copies.append(
            pltpu.make_async_copy(
                held.at[j, :, :width], out_ref.at[:, at : at + width], sems.at[1, j]
            )
        )
    for fetch in fetches:
        fetch.start()
    for fetch, copy in zip(fetches, copies, strict=True):
        fetch.wait()
        copy.start()
    if with_latents:
        total = held[0, :, width:].astype(jnp.float32)
        for j in range(1, groups):
            total += held[j, :, width:].astype(jnp.float32)
        refs[2][...] = total.T[: LATENT + ROPE].astype(part_ref.dtype)
    for copy in copies:
        copy.wait()


def unpack(total, part, first, pairs, per_group, with_latents):
    groups, tokens, _ = part.shape
    hbm = pl.BlockSpec(memory_space=pl.ANY)
    out_specs = [hbm]
    shapes = [jax.ShapeDtypeStruct((tokens, groups * per_group * QPAIR), part.dtype)]
    if with_latents:
        out_specs.append(pl.BlockSpec(memory_space=pltpu.VMEM))
        shapes.append(jax.ShapeDtypeStruct((LATENT + ROPE, tokens), part.dtype))
    has = total is not None
    return pl.pallas_call(
        functools.partial(unpack_kernel, first, pairs, has, with_latents),
        in_specs=[hbm] * (1 + has),
        out_specs=out_specs,
        out_shape=shapes,
        scratch_shapes=[
            pltpu.SemaphoreType.DMA((2, groups)),
            pltpu.VMEM(part.shape, part.dtype),
        ],
        input_output_aliases={0: 0} if has else {},
        compiler_params=pltpu.CompilerParams(vmem_limit_bytes=VMEM),
        cost_estimate=SMALL,
        name="unpack",
    )(*([total] * has + [part]))


def scores_of(head, first, limit):
    q_ref, q_at, g_ref, g_at, key, value = head[:6]
    q = q_ref[first:limit, q_at : q_at + 256]
    g = g_ref[first:limit, g_at : g_at + VDIM]
    scores = dot(key[:limit], q, ((1,), (1,)))
    return scores, dot(value[:limit], g, ((1,), (1,))), q, g


def two_heads(heads, scale, block):
    span = heads[0][4].shape[0]
    steps = [(n, at) for at in reversed(range(span // block)) for n in range(len(heads))]
    dq_rows = [[] for _ in heads]
    ahead = scores_of(heads[0], steps[0][1] * block, (steps[0][1] + 1) * block)
    for number, (n, index) in enumerate(steps):
        first, limit = index * block, (index + 1) * block
        scores, dprobs, q, g = ahead
        if number + 1 < len(steps):
            after_n, after_at = steps[number + 1]
            ahead = scores_of(heads[after_n], after_at * block, (after_at + 1) * block)
        key, dk_ref, dv_ref = heads[n][4], heads[n][6], heads[n][7]
        key_pos = lax.broadcasted_iota(jnp.int32, (block, block), 0)
        query_pos = lax.broadcasted_iota(jnp.int32, (block, block), 1)
        last = jnp.where(key_pos <= query_pos, scores[first:], -jnp.inf)
        scores = jnp.concatenate([scores[:first], last], axis=0) if index else last
        top = jnp.max(scores, axis=0, keepdims=True)
        expo = jnp.exp2((scores - top) * (scale * LOG2E))
        probs = expo * (1.0 / jnp.sum(expo, axis=0, keepdims=True))
        delta = jnp.sum(probs * dprobs, axis=0, keepdims=True)
        dscores = (probs * (dprobs - delta)).astype(jnp.bfloat16)
        dv = dot(probs.astype(jnp.bfloat16), g, ((1,), (0,)))
        dk = dot(dscores, q, ((1,), (0,)))
        if limit == span:
            dv_ref[...] = dv
            dk_ref[...] = dk
        else:
            dv_ref[:limit] += dv
            dk_ref[:limit] += dk
        dq_rows[n].append(dot(dscores, key[:limit], ((0,), (0,))))
    return [jnp.concatenate(rows[::-1], axis=0) for rows in dq_rows]


def attend_kernel(pairs, has_sum, last, *refs):
    refs = list(refs)
    place, lat_ref, w_ref, q_ref = refs[:4]
    rest = refs[4:]
    if pairs == 1:
        q_ref, g_ref = q_ref.at[:, :QPAIR], q_ref.at[:, QPAIR:]
    else:
        g_ref = rest.pop(0)
    sum_in = rest.pop(0) if has_sum else None
    if last:
        dq_ref, keep_ref, send_ref, total, dk0, dv0, dk1, dv1 = rest
        dq_ref, out_ref = dq_ref.at[:, :QPAIR], dq_ref.at[:, QPAIR:]
    else:
        dq_ref, keep_ref, send_ref, out_ref, total, dk0, dv0, dk1, dv1 = rest
    step = pl.program_id(0)
    scale = (NOPE + ROPE) ** (-0.5)
    half = NOPE // 2
    span = lat_ref.shape[0]
    block = min(256, span)
    plain = lat_ref[:, :LATENT]
    rope = lat_ref[:, LATENT:]
    keyval = dot(plain, w_ref[...], ((1,), (0,)))
    lane = lax.broadcasted_iota(jnp.int32, (span, NOPE), 1)
    key0 = jnp.concatenate([keyval[:, :NOPE].astype(jnp.bfloat16), rope], axis=1)
    value0 = keyval[:, NOPE : 2 * NOPE].astype(jnp.bfloat16)
    moved = pltpu.roll(keyval[:, 2 * NOPE : 3 * NOPE], half, 1)
    rope_moved = pltpu.roll(rope.astype(jnp.float32), half, 1)
    key1 = jnp.concatenate(
        [jnp.where(lane < half, 0.0, moved), jnp.where(lane < half, moved, rope_moved)], axis=1
    ).astype(jnp.bfloat16)
    value1 = keyval[:, 3 * NOPE :].astype(jnp.bfloat16)
    dq0, dq1 = two_heads(
        [
            (q_ref, 0, g_ref, 0, key0, value0, dk0, dv0),
            (q_ref, NOPE, g_ref, VDIM, key1, value1, dk1, dv1),
        ],
        scale,
        block,
    )
    dq = jnp.concatenate([dq0[:, :NOPE], dq0[:, NOPE:] + dq1[:, :NOPE], dq1[:, NOPE:]], axis=1)
    dq = (dq * scale).astype(jnp.bfloat16)
    dq_ref[...] = dq
    left = pltpu.roll(dk1[:, :NOPE], half, 1)
    right = pltpu.roll(dk1[:, NOPE:], half, 1)
    dkeyval = jnp.concatenate(
        [
            dk0[:, :NOPE] * scale,
            dv0[...],
            jnp.where(lane < half, left, right) * scale,
            dv1[...],
        ],
        axis=1,
    ).astype(jnp.bfloat16)
    drope = jnp.where(lane < half, (dk0[:, NOPE:] + right) * scale, 0.0)
    back = dot(dkeyval, w_ref[...], ((1,), (1,)))
    dw = dot(plain, dkeyval, ((0,), (0,))).astype(jnp.bfloat16)
    rows = LATENT // 2 // LINE
    for at in range(2 * LINE):
        to = lax.rem(at % LINE - place[1] + LINE, LINE)
        to = pl.ds(pl.multiple_of(to * rows, rows), rows)
        piece = dw[at * rows : (at + 1) * rows]

        @pl.when(place[0] == at // LINE)
        def _():
            keep_ref[to, :] = piece

        @pl.when(place[0] != at // LINE)
        def _():
            send_ref[to, :] = piece

    @pl.when(step == 0)
    def _():
        if has_sum:
            total[:, :LATENT] = back + sum_in[:, :LATENT]
            total[:, LATENT:] = drope + sum_in[:, LATENT:]
        else:
            total[:, :LATENT] = back
            total[:, LATENT:] = drope

    @pl.when(step > 0)
    def _():
        total[:, :LATENT] += back
        total[:, LATENT:] += drope

    @pl.when(step == pl.num_programs(0) - 1)
    def _():
        out_ref[...] = total[...].astype(out_ref.dtype)


def attend(place, lat, lat_block, weight, first, x, pairs, total, last):
    span = lat.shape[0]
    f32, bf16 = jnp.float32, jnp.bfloat16
    whole = lambda j: (0, 0)
    column = lambda j: (0, j)
    specs = [
        pl.BlockSpec(memory_space=pltpu.SMEM),
        pl.BlockSpec((span, LATPAD), lambda j: (0, lat_block)),
        pl.BlockSpec((LATENT, KVPAIR), lambda j: (0, first + j)),
    ]
    args = [place, lat, weight, x]
    if pairs == 1:
        specs.append(pl.BlockSpec((span, PAIR), whole))
    else:
        specs.append(pl.BlockSpec((span, QPAIR), lambda j: (0, pairs * GPAIR // QPAIR + j)))
        specs.append(pl.BlockSpec((span, GPAIR), column))
        args.append(x)
    if total is not None:
        specs.append(pl.BlockSpec((span, LATPAD), whole))
        args.append(total)
    dw_shape = jax.ShapeDtypeStruct((LATENT // 2, pairs * KVPAIR), bf16)
    out_specs = [pl.BlockSpec((LATENT // 2, KVPAIR), column)] * 2
    shapes = [dw_shape, dw_shape]
    if last:
        out_specs = [pl.BlockSpec((span, QPAIR + LATPAD), whole)] + out_specs
        shapes = [jax.ShapeDtypeStruct((span, QPAIR + LATPAD), bf16)] + shapes
    else:
        out_specs = [pl.BlockSpec((span, QPAIR), column)] + out_specs
        shapes = [jax.ShapeDtypeStruct((span, pairs * QPAIR), bf16)] + shapes
        out_specs.append(pl.BlockSpec((span, LATPAD), whole))
        shapes.append(jax.ShapeDtypeStruct((span, LATPAD), f32))
    return pl.pallas_call(
        functools.partial(attend_kernel, pairs, total is not None, last),
        grid=(pairs,),
        in_specs=specs,
        out_specs=out_specs,
        out_shape=shapes,
        scratch_shapes=[
            pltpu.VMEM((span, LATPAD), f32),
            pltpu.VMEM((span, 2 * NOPE), f32),
            pltpu.VMEM((span, VDIM), f32),
            pltpu.VMEM((span, 2 * NOPE), f32),
            pltpu.VMEM((span, VDIM), f32),
        ],
        compiler_params=pltpu.CompilerParams(vmem_limit_bytes=VMEM),
        cost_estimate=pl.CostEstimate(
            flops=pairs * 5_000_000_000, bytes_accessed=pairs * 6_000_000, transcendentals=0
        ),
        name="attend",
    )(*args)


def exchange(x, axis, groups=None):
    return lax.all_to_all(x, axis, split_axis=0, concat_axis=0, tiled=True, axis_index_groups=groups)


def send(x, step):
    slabs = lax.axis_size("dp")
    return lax.ppermute(x, "dp", [(i, step(i)) for i in range(slabs)])


def along(step):
    def to(i):
        near = 2 * LINE
        return i // near * near + ((i // 2 + step) % LINE) * 2 + i % 2

    return to


def add_kernel(*refs):
    *parts, out_ref = refs
    total = parts[0][...].astype(jnp.float32)
    for part in parts[1:]:
        total += part[...].astype(jnp.float32)
    out_ref[...] = total.astype(out_ref.dtype)


def add(*parts):
    cost = pl.CostEstimate(flops=ADD_FLOPS, bytes_accessed=1, transcendentals=0)
    return pl.pallas_call(add_kernel, out_shape=parts[0], cost_estimate=cost, name="add")(*parts)


def split_kernel(keep_ref, got_ref, *out_refs):
    total = keep_ref[...].astype(jnp.float32) + got_ref[...].astype(jnp.float32)
    rows = out_refs[0].shape[0]
    for index, out_ref in enumerate(out_refs):
        out_ref[...] = total[index * rows : (index + 1) * rows].astype(out_ref.dtype)


def split(keep, got):
    shape = jax.ShapeDtypeStruct((keep.shape[0] // LINE, keep.shape[1]), keep.dtype)
    shapes = [shape] * LINE
    return pl.pallas_call(split_kernel, out_shape=shapes, cost_estimate=SMALL, name="split")(
        keep, got
    )


def swap(x):
    return send(x, lambda i: i ^ 1)


def spread(pieces):
    return [pieces[0]] + [send(x, along(k + 1)) for k, x in enumerate(pieces[1:])]


def merge_kernel(count, *refs):
    *parts, out_ref = refs
    at = 0
    for group in (parts[:count], parts[count:]):
        total = group[0][...].astype(jnp.float32)
        for part in group[1:]:
            total += part[...].astype(jnp.float32)
        out_ref[:, at : at + total.shape[1]] = total.astype(out_ref.dtype)
        at += total.shape[1]


def merge(first, second):
    rows = first[0].shape[0]
    shape = jax.ShapeDtypeStruct((rows, first[0].shape[1] + second[0].shape[1]), first[0].dtype)
    kernel = functools.partial(merge_kernel, len(first))
    return pl.pallas_call(kernel, out_shape=shape, cost_estimate=SMALL, name="merge")(
        *first, *second
    )


def across(part):
    slabs = 4 * LINE
    return send(part, lambda i: (i + slabs // 2) % slabs)


def place_kernel(slabs, place, *refs):
    *parts, out_ref = refs
    rows = parts[0].shape[0]
    for ref, core, k in zip(parts, [0] * LINE + [1] * LINE, 2 * list(range(LINE)), strict=True):
        core = 1 - place[0] if core else place[0]
        at = core * LINE + lax.rem(place[1] - k + LINE, LINE)
        to = pl.ds(pl.multiple_of(at * rows, rows), rows)
        out_ref[to, :] = ref[...].astype(jnp.float32) * (1.0 / slabs)


def place_slabs(place, mine, other):
    vmem = pl.BlockSpec(memory_space=pltpu.VMEM)
    return pl.pallas_call(
        functools.partial(place_kernel, lax.axis_size("dp")),
        in_specs=[pl.BlockSpec(memory_space=pltpu.SMEM)] + [vmem] * (2 * LINE),
        out_specs=vmem,
        out_shape=jax.ShapeDtypeStruct((LATENT, mine[0].shape[1]), jnp.float32),
        compiler_params=pltpu.CompilerParams(vmem_limit_bytes=VMEM),
        cost_estimate=SMALL,
        name="place",
    )(place, *mine, *other)


def after(x, *others):
    return lax.optimization_barrier((x,) + others)


def shards(queries, latents, kv_weight, out_grad):
    groups = lax.axis_size("seq")
    tokens = queries.shape[1]
    span = tokens * groups
    per_group = kv_weight.shape[1] // KVPAIR
    late = per_group - EARLY
    q, g, lat = queries[0], out_grad[0], latents[0].T
    me = lax.axis_index("dp")
    place = jnp.stack([me % 2, me // 2 % LINE]).astype(jnp.int32)

    x0, x1 = pack(q, g, lat, groups, ((0, EARLY), (EARLY, late)))
    x0, place = after(x0, place)
    got0 = exchange(x0, "seq")
    x1, got0 = after(x1, got0)
    got1 = exchange(x1, "seq")
    lat = got0.reshape(span, got0.shape[2])
    kv = (place, lat, EARLY * PAIR // LATPAD, kv_weight)
    dq0, keep0, give0, total = attend(*kv, 0, lat, EARLY, None, False)
    back0 = exchange(dq0.reshape(groups, tokens, EARLY * QPAIR), "seq")
    swap0 = swap(give0)
    send1, keep1, give1 = attend(*kv, EARLY, got1.reshape(span, PAIR), late, total, True)
    send1, keep1, give1, keep0, swap0 = after(send1, keep1, give1, keep0, swap0)
    pieces0 = spread(split(keep0, swap0))
    pieces1 = spread(split(keep1, swap(give1)))
    part = merge(pieces0, pieces1)
    other = across(part)
    (query_grad,) = unpack(None, back0, 0, EARLY, per_group, False)
    send1, query_grad, part = after(send1, query_grad, part)
    back1 = exchange(send1.reshape(groups, tokens, QPAIR + LATPAD), "seq")
    line = spread([add(part, other)] * LINE)
    weight_grad = place_slabs(place, line, [swap(x) for x in line])
    query_grad, latent_grad = unpack(query_grad, back1, EARLY, late, per_group, True)
    return (query_grad[None], latent_grad.T[None], weight_grad)


def solution(mesh):
    placed = (P("dp", "seq", None), P("dp", "seq", None), P(None, "seq"), P("dp", "seq", None))
    return jax.shard_map(
        shards,
        mesh=mesh,
        in_specs=placed,
        out_specs=(P("dp", "seq", None), P("dp", "seq", None), P(None, "seq")),
        check_vma=False,
    )
```

```python
import functools

import jax
import jax.numpy as jnp
from jax import lax
from jax.experimental import pallas as pl
from jax.experimental.pallas import tpu as pltpu
from jax.sharding import PartitionSpec as P

NOPE = 128
ROPE = 64
VDIM = 128
LATENT = 512
QPAIR = 2 * (NOPE + ROPE)
GPAIR = 2 * VDIM
PAIR = QPAIR + GPAIR
KVPAIR = 2 * (NOPE + VDIM)
LATPAD = 640
LOG2E = 1.4426950408889634
VMEM = 56 * 1024 * 1024
SMALL = pl.CostEstimate(flops=1, bytes_accessed=1, transcendentals=0)
EARLY = 3
LINE = 4
ADD_FLOPS = 40_000_000_000


def dot(a, b, dims):
    return lax.dot_general(a, b, (dims, ((), ())), preferred_element_type=jnp.float32)


def places(pairs):
    return (0, QPAIR) if pairs == 1 else (pairs * GPAIR, 0)


def pack_kernel(plans, q_ref, g_ref, lat_ref, *refs):
    count = len(plans)
    outs, held, sems, sent = refs[:count], refs[count : 2 * count], refs[-2], refs[-1]
    groups = outs[0].shape[0]
    per_group = q_ref.shape[1] // (groups * QPAIR)
    batches, number = [], 0
    for n, (first, pairs) in enumerate(plans):
        for j in range(groups):
            batch = []
            at = j * per_group + first
            q_at, g_at = places(pairs)
            for ref, width, to in ((q_ref, QPAIR, q_at), (g_ref, GPAIR, g_at)):
                batch.append(
                    pltpu.make_async_copy(
                        ref.at[:, at * width : (at + pairs) * width],
                        held[n].at[j, :, to : to + pairs * width],
                        sems.at[number],
                    )
                )
                number += 1
            leave = pltpu.make_async_copy(held[n].at[j], outs[n].at[j], sent.at[n, j])
            batches.append((batch, leave))
    for batch, _ in batches:
        for copy in batch:
            copy.start()
    base = plans[0][1] * PAIR
    rows = lat_ref[...].T
    pad = jnp.zeros((rows.shape[0], LATPAD - rows.shape[1]), rows.dtype)
    rows = jnp.concatenate([rows, pad], axis=1)
    for j in range(groups):
        held[0][j, :, base:] = rows
    for batch, leave in batches:
        for copy in batch:
            copy.wait()
        leave.start()
    for _, leave in batches:
        leave.wait()


def pack(q, g, latents, groups, plans):
    tokens = q.shape[0]
    hbm = pl.BlockSpec(memory_space=pl.ANY)
    shapes = []
    for index, (_, pairs) in enumerate(plans):
        width = pairs * PAIR + (LATPAD if index == 0 else 0)
        shapes.append(jax.ShapeDtypeStruct((groups, tokens, width), q.dtype))
    return pl.pallas_call(
        functools.partial(pack_kernel, plans),
        in_specs=[hbm, hbm, pl.BlockSpec(memory_space=pltpu.VMEM)],
        out_specs=[hbm] * len(plans),
        out_shape=shapes,
        scratch_shapes=[pltpu.VMEM(shape.shape, shape.dtype) for shape in shapes]
        + [
            pltpu.SemaphoreType.DMA((2 * groups * len(plans),)),
            pltpu.SemaphoreType.DMA((len(plans), groups)),
        ],
        compiler_params=pltpu.CompilerParams(vmem_limit_bytes=VMEM),
        cost_estimate=pl.CostEstimate(
            flops=0, bytes_accessed=sum(4 * s.size for s in shapes), transcendentals=0
        ),
        name="pack",
    )(q, g, latents)


def unpack_kernel(first, pairs, has_total, with_latents, *refs):
    refs = list(refs)
    if has_total:
        refs.pop(0)
    part_ref, out_ref = refs[:2]
    groups = part_ref.shape[0]
    per_group = out_ref.shape[1] // (groups * QPAIR)
    width = pairs * QPAIR
    sems, held = refs[-2:]
    fetches, copies = [], []
    for j in range(groups):
        at = (j * per_group + first) * QPAIR
        fetches.append(pltpu.make_async_copy(part_ref.at[j], held.at[j], sems.at[0, j]))
        copies.append(
            pltpu.make_async_copy(
                held.at[j, :, :width], out_ref.at[:, at : at + width], sems.at[1, j]
            )
        )
    for fetch in fetches:
        fetch.start()
    for fetch, copy in zip(fetches, copies, strict=True):
        fetch.wait()
        copy.start()
    if with_latents:
        total = held[0, :, width:].astype(jnp.float32)
        for j in range(1, groups):
            total += held[j, :, width:].astype(jnp.float32)
        refs[2][...] = total.T[: LATENT + ROPE].astype(part_ref.dtype)
    for copy in copies:
        copy.wait()


def unpack(total, part, first, pairs, per_group, with_latents):
    groups, tokens, _ = part.shape
    hbm = pl.BlockSpec(memory_space=pl.ANY)
    out_specs = [hbm]
    shapes = [jax.ShapeDtypeStruct((tokens, groups * per_group * QPAIR), part.dtype)]
    if with_latents:
        out_specs.append(pl.BlockSpec(memory_space=pltpu.VMEM))
        shapes.append(jax.ShapeDtypeStruct((LATENT + ROPE, tokens), part.dtype))
    has = total is not None
    return pl.pallas_call(
        functools.partial(unpack_kernel, first, pairs, has, with_latents),
        in_specs=[hbm] * (1 + has),
        out_specs=out_specs,
        out_shape=shapes,
        scratch_shapes=[
            pltpu.SemaphoreType.DMA((2, groups)),
            pltpu.VMEM(part.shape, part.dtype),
        ],
        input_output_aliases={0: 0} if has else {},
        compiler_params=pltpu.CompilerParams(vmem_limit_bytes=VMEM // 4),
        cost_estimate=SMALL,
        name="unpack",
    )(*([total] * has + [part]))


def scores_of(head, first, limit):
    q_ref, q_at, g_ref, g_at, key, value = head[:6]
    q = q_ref[first:limit, q_at : q_at + 256]
    g = g_ref[first:limit, g_at : g_at + VDIM]
    scores = dot(key[:limit], q, ((1,), (1,)))
    return scores, dot(value[:limit], g, ((1,), (1,))), q, g


def two_heads(heads, scale, block):
    span = heads[0][4].shape[0]
    steps = [(n, at) for at in reversed(range(span // block)) for n in range(len(heads))]
    dq_rows = [[] for _ in heads]
    ahead = scores_of(heads[0], steps[0][1] * block, (steps[0][1] + 1) * block)
    for number, (n, index) in enumerate(steps):
        first, limit = index * block, (index + 1) * block
        scores, dprobs, q, g = ahead
        if number + 1 < len(steps):
            after_n, after_at = steps[number + 1]
            ahead = scores_of(heads[after_n], after_at * block, (after_at + 1) * block)
        key, dk_ref, dv_ref = heads[n][4], heads[n][6], heads[n][7]
        key_pos = lax.broadcasted_iota(jnp.int32, (block, block), 0)
        query_pos = lax.broadcasted_iota(jnp.int32, (block, block), 1)
        last = jnp.where(key_pos <= query_pos, scores[first:], -jnp.inf)
        scores = jnp.concatenate([scores[:first], last], axis=0) if index else last
        top = jnp.max(scores, axis=0, keepdims=True)
        expo = jnp.exp2((scores - top) * (scale * LOG2E))
        probs = expo * (1.0 / jnp.sum(expo, axis=0, keepdims=True))
        delta = jnp.sum(probs * dprobs, axis=0, keepdims=True)
        dscores = (probs * (dprobs - delta)).astype(jnp.bfloat16)
        dv = dot(probs.astype(jnp.bfloat16), g, ((1,), (0,)))
        dk = dot(dscores, q, ((1,), (0,)))
        if limit == span:
            dv_ref[...] = dv
            dk_ref[...] = dk
        else:
            dv_ref[:limit] += dv
            dk_ref[:limit] += dk
        dq_rows[n].append(dot(dscores, key[:limit], ((0,), (0,))))
    return [jnp.concatenate(rows[::-1], axis=0) for rows in dq_rows]


def attend_kernel(pairs, has_sum, last, *refs):
    refs = list(refs)
    place, lat_ref, w_ref, q_ref = refs[:4]
    rest = refs[4:]
    if pairs == 1:
        q_ref, g_ref = q_ref.at[:, :QPAIR], q_ref.at[:, QPAIR:]
    else:
        g_ref = rest.pop(0)
    sum_in = rest.pop(0) if has_sum else None
    if last:
        dq_ref, keep_ref, send_ref, total, dk0, dv0, dk1, dv1 = rest
        dq_ref, out_ref = dq_ref.at[:, :QPAIR], dq_ref.at[:, QPAIR:]
    else:
        dq_ref, keep_ref, send_ref, out_ref, total, dk0, dv0, dk1, dv1 = rest
    step = pl.program_id(0)
    scale = (NOPE + ROPE) ** (-0.5)
    half = NOPE // 2
    span = lat_ref.shape[0]
    block = min(256, span)
    plain = lat_ref[:, :LATENT]
    rope = lat_ref[:, LATENT:]
    keyval = dot(plain, w_ref[...], ((1,), (0,)))
    lane = lax.broadcasted_iota(jnp.int32, (span, NOPE), 1)
    key0 = jnp.concatenate([keyval[:, :NOPE].astype(jnp.bfloat16), rope], axis=1)
    value0 = keyval[:, NOPE : 2 * NOPE].astype(jnp.bfloat16)
    moved = pltpu.roll(keyval[:, 2 * NOPE : 3 * NOPE], half, 1)
    rope_moved = pltpu.roll(rope.astype(jnp.float32), half, 1)
    key1 = jnp.concatenate(
        [jnp.where(lane < half, 0.0, moved), jnp.where(lane < half, moved, rope_moved)], axis=1
    ).astype(jnp.bfloat16)
    value1 = keyval[:, 3 * NOPE :].astype(jnp.bfloat16)
    dq0, dq1 = two_heads(
        [
            (q_ref, 0, g_ref, 0, key0, value0, dk0, dv0),
            (q_ref, NOPE, g_ref, VDIM, key1, value1, dk1, dv1),
        ],
        scale,
        block,
    )
    dq = jnp.concatenate([dq0[:, :NOPE], dq0[:, NOPE:] + dq1[:, :NOPE], dq1[:, NOPE:]], axis=1)
    dq = (dq * scale).astype(jnp.bfloat16)
    dq_ref[...] = dq
    left = pltpu.roll(dk1[:, :NOPE], half, 1)
    right = pltpu.roll(dk1[:, NOPE:], half, 1)
    dkeyval = jnp.concatenate(
        [
            dk0[:, :NOPE] * scale,
            dv0[...],
            jnp.where(lane < half, left, right) * scale,
            dv1[...],
        ],
        axis=1,
    ).astype(jnp.bfloat16)
    drope = jnp.where(lane < half, (dk0[:, NOPE:] + right) * scale, 0.0)
    back = dot(dkeyval, w_ref[...], ((1,), (1,)))
    dw = dot(plain, dkeyval, ((0,), (0,))).astype(jnp.bfloat16)
    rows = LATENT // 2 // LINE
    for at in range(2 * LINE):
        to = lax.rem(at % LINE - place[1] + LINE, LINE)
        to = pl.ds(pl.multiple_of(to * rows, rows), rows)
        piece = dw[at * rows : (at + 1) * rows]

        @pl.when(place[0] == at // LINE)
        def _():
            keep_ref[to, :] = piece

        @pl.when(place[0] != at // LINE)
        def _():
            send_ref[to, :] = piece

    @pl.when(step == 0)
    def _():
        if has_sum:
            total[:, :LATENT] = back + sum_in[:, :LATENT]
            total[:, LATENT:] = drope + sum_in[:, LATENT:]
        else:
            total[:, :LATENT] = back
            total[:, LATENT:] = drope

    @pl.when(step > 0)
    def _():
        total[:, :LATENT] += back
        total[:, LATENT:] += drope

    @pl.when(step == pl.num_programs(0) - 1)
    def _():
        out_ref[...] = total[...].astype(out_ref.dtype)


def attend(place, lat, lat_block, weight, first, x, pairs, total, last):
    span = lat.shape[0]
    f32, bf16 = jnp.float32, jnp.bfloat16
    whole = lambda j: (0, 0)
    column = lambda j: (0, j)
    specs = [
        pl.BlockSpec(memory_space=pltpu.SMEM),
        pl.BlockSpec((span, LATPAD), lambda j: (0, lat_block)),
        pl.BlockSpec((LATENT, KVPAIR), lambda j: (0, first + j)),
    ]
    args = [place, lat, weight, x]
    if pairs == 1:
        specs.append(pl.BlockSpec((span, PAIR), whole))
    else:
        specs.append(pl.BlockSpec((span, QPAIR), lambda j: (0, pairs * GPAIR // QPAIR + j)))
        specs.append(pl.BlockSpec((span, GPAIR), column))
        args.append(x)
    if total is not None:
        specs.append(pl.BlockSpec((span, LATPAD), whole))
        args.append(total)
    dw_shape = jax.ShapeDtypeStruct((LATENT // 2, pairs * KVPAIR), bf16)
    out_specs = [pl.BlockSpec((LATENT // 2, KVPAIR), column)] * 2
    shapes = [dw_shape, dw_shape]
    if last:
        out_specs = [pl.BlockSpec((span, QPAIR + LATPAD), whole)] + out_specs
        shapes = [jax.ShapeDtypeStruct((span, QPAIR + LATPAD), bf16)] + shapes
    else:
        out_specs = [pl.BlockSpec((span, QPAIR), column)] + out_specs
        shapes = [jax.ShapeDtypeStruct((span, pairs * QPAIR), bf16)] + shapes
        out_specs.append(pl.BlockSpec((span, LATPAD), whole))
        shapes.append(jax.ShapeDtypeStruct((span, LATPAD), f32))
    return pl.pallas_call(
        functools.partial(attend_kernel, pairs, total is not None, last),
        grid=(pairs,),
        in_specs=specs,
        out_specs=out_specs,
        out_shape=shapes,
        scratch_shapes=[
            pltpu.VMEM((span, LATPAD), f32),
            pltpu.VMEM((span, 2 * NOPE), f32),
            pltpu.VMEM((span, VDIM), f32),
            pltpu.VMEM((span, 2 * NOPE), f32),
            pltpu.VMEM((span, VDIM), f32),
        ],
        compiler_params=pltpu.CompilerParams(vmem_limit_bytes=VMEM),
        cost_estimate=pl.CostEstimate(
            flops=pairs * 5_000_000_000, bytes_accessed=pairs * 6_000_000, transcendentals=0
        ),
        name="attend",
    )(*args)


def exchange(x, axis, groups=None):
    return lax.all_to_all(x, axis, split_axis=0, concat_axis=0, tiled=True, axis_index_groups=groups)


def send(x, step):
    slabs = lax.axis_size("dp")
    return lax.ppermute(x, "dp", [(i, step(i)) for i in range(slabs)])


def along(step):
    def to(i):
        near = 2 * LINE
        return i // near * near + ((i // 2 + step) % LINE) * 2 + i % 2

    return to


def add_kernel(*refs):
    *parts, out_ref = refs
    total = parts[0][...].astype(jnp.float32)
    for part in parts[1:]:
        total += part[...].astype(jnp.float32)
    out_ref[...] = total.astype(out_ref.dtype)


def add(*parts):
    cost = pl.CostEstimate(flops=ADD_FLOPS, bytes_accessed=1, transcendentals=0)
    return pl.pallas_call(add_kernel, out_shape=parts[0], cost_estimate=cost, name="add")(*parts)


def split_kernel(keep_ref, got_ref, *out_refs):
    total = keep_ref[...].astype(jnp.float32) + got_ref[...].astype(jnp.float32)
    rows = out_refs[0].shape[0]
    for index, out_ref in enumerate(out_refs):
        out_ref[...] = total[index * rows : (index + 1) * rows].astype(out_ref.dtype)


def split(keep, got):
    shape = jax.ShapeDtypeStruct((keep.shape[0] // LINE, keep.shape[1]), keep.dtype)
    shapes = [shape] * LINE
    return pl.pallas_call(split_kernel, out_shape=shapes, cost_estimate=SMALL, name="split")(
        keep, got
    )


def swap(x):
    return send(x, lambda i: i ^ 1)


def spread(pieces):
    return [pieces[0]] + [send(x, along(k + 1)) for k, x in enumerate(pieces[1:])]


def merge_kernel(count, *refs):
    *parts, out_ref = refs
    at = 0
    for group in (parts[:count], parts[count:]):
        total = group[0][...].astype(jnp.float32)
        for part in group[1:]:
            total += part[...].astype(jnp.float32)
        out_ref[:, at : at + total.shape[1]] = total.astype(out_ref.dtype)
        at += total.shape[1]


def merge(first, second):
    rows = first[0].shape[0]
    shape = jax.ShapeDtypeStruct((rows, first[0].shape[1] + second[0].shape[1]), first[0].dtype)
    kernel = functools.partial(merge_kernel, len(first))
    return pl.pallas_call(kernel, out_shape=shape, cost_estimate=SMALL, name="merge")(
        *first, *second
    )


def across(part):
    slabs = 4 * LINE
    return send(part, lambda i: (i + slabs // 2) % slabs)


def place_kernel(slabs, place, *refs):
    *parts, out_ref = refs
    rows = parts[0].shape[0]
    for ref, core, k in zip(parts, [0] * LINE + [1] * LINE, 2 * list(range(LINE)), strict=True):
        core = 1 - place[0] if core else place[0]
        at = core * LINE + lax.rem(place[1] - k + LINE, LINE)
        to = pl.ds(pl.multiple_of(at * rows, rows), rows)
        out_ref[to, :] = ref[...].astype(jnp.float32) * (1.0 / slabs)


def place_slabs(place, mine, other):
    vmem = pl.BlockSpec(memory_space=pltpu.VMEM)
    return pl.pallas_call(
        functools.partial(place_kernel, lax.axis_size("dp")),
        in_specs=[pl.BlockSpec(memory_space=pltpu.SMEM)] + [vmem] * (2 * LINE),
        out_specs=vmem,
        out_shape=jax.ShapeDtypeStruct((LATENT, mine[0].shape[1]), jnp.float32),
        compiler_params=pltpu.CompilerParams(vmem_limit_bytes=VMEM),
        cost_estimate=SMALL,
        name="place",
    )(place, *mine, *other)


def after(x, *others):
    return lax.optimization_barrier((x,) + others)


def shards(queries, latents, kv_weight, out_grad):
    groups = lax.axis_size("seq")
    tokens = queries.shape[1]
    span = tokens * groups
    per_group = kv_weight.shape[1] // KVPAIR
    late = per_group - EARLY
    q, g, lat = queries[0], out_grad[0], latents[0].T
    me = lax.axis_index("dp")
    place = jnp.stack([me % 2, me // 2 % LINE]).astype(jnp.int32)

    x0, x1 = pack(q, g, lat, groups, ((0, EARLY), (EARLY, late)))
    x0, place = after(x0, place)
    got0 = exchange(x0, "seq")
    x1, got0 = after(x1, got0)
    got1 = exchange(x1, "seq")
    lat = got0.reshape(span, got0.shape[2])
    kv = (place, lat, EARLY * PAIR // LATPAD, kv_weight)
    dq0, keep0, give0, total = attend(*kv, 0, lat, EARLY, None, False)
    back0 = exchange(dq0.reshape(groups, tokens, EARLY * QPAIR), "seq")
    swap0 = swap(give0)
    send1, keep1, give1 = attend(*kv, EARLY, got1.reshape(span, PAIR), late, total, True)
    send1, keep1, give1, keep0, swap0 = after(send1, keep1, give1, keep0, swap0)
    pieces0 = spread(split(keep0, swap0))
    pieces1 = spread(split(keep1, swap(give1)))
    part = merge(pieces0, pieces1)
    other = across(part)
    (query_grad,) = unpack(None, back0, 0, EARLY, per_group, False)
    send1, query_grad, part = after(send1, query_grad, part)
    back1 = exchange(send1.reshape(groups, tokens, QPAIR + LATPAD), "seq")
    line = spread([add(part, other)] * LINE)
    weight_grad = place_slabs(place, line, [swap(x) for x in line])
    query_grad, latent_grad = unpack(query_grad, back1, EARLY, late, per_group, True)
    return (query_grad[None], latent_grad.T[None], weight_grad)


def solution(mesh):
    placed = (P("dp", "seq", None), P("dp", "seq", None), P(None, "seq"), P("dp", "seq", None))
    return jax.shard_map(
        shards,
        mesh=mesh,
        in_specs=placed,
        out_specs=(P("dp", "seq", None), P("dp", "seq", None), P(None, "seq")),
        check_vma=False,
    )
```

```python
import functools

import jax
import jax.numpy as jnp
from jax import lax
from jax.experimental import pallas as pl
from jax.experimental.pallas import tpu as pltpu
from jax.sharding import PartitionSpec as P

NOPE = 128
ROPE = 64
VDIM = 128
LATENT = 512
QPAIR = 2 * (NOPE + ROPE)
GPAIR = 2 * VDIM
PAIR = QPAIR + GPAIR
KVPAIR = 2 * (NOPE + VDIM)
LATPAD = 640
LOG2E = 1.4426950408889634
VMEM = 56 * 1024 * 1024
LITTLE = pltpu.CompilerParams(vmem_limit_bytes=VMEM // 4)
SMALL = pl.CostEstimate(flops=1, bytes_accessed=1, transcendentals=0)
EARLY = 3
LINE = 4
ADD_FLOPS = 40_000_000_000


def dot(a, b, dims):
    return lax.dot_general(a, b, (dims, ((), ())), preferred_element_type=jnp.float32)


def places(pairs):
    return (0, QPAIR) if pairs == 1 else (pairs * GPAIR, 0)


def pack_kernel(plans, q_ref, g_ref, lat_ref, *refs):
    count = len(plans)
    outs, held, sems, sent = refs[:count], refs[count : 2 * count], refs[-2], refs[-1]
    groups = outs[0].shape[0]
    per_group = q_ref.shape[1] // (groups * QPAIR)
    batches, number = [], 0
    for n, (first, pairs) in enumerate(plans):
        for j in range(groups):
            batch = []
            at = j * per_group + first
            q_at, g_at = places(pairs)
            for ref, width, to in ((q_ref, QPAIR, q_at), (g_ref, GPAIR, g_at)):
                batch.append(
                    pltpu.make_async_copy(
                        ref.at[:, at * width : (at + pairs) * width],
                        held[n].at[j, :, to : to + pairs * width],
                        sems.at[number],
                    )
                )
                number += 1
            leave = pltpu.make_async_copy(held[n].at[j], outs[n].at[j], sent.at[n, j])
            batches.append((batch, leave))
    for batch, _ in batches:
        for copy in batch:
            copy.start()
    base = plans[0][1] * PAIR
    rows = lat_ref[...].T
    pad = jnp.zeros((rows.shape[0], LATPAD - rows.shape[1]), rows.dtype)
    rows = jnp.concatenate([rows, pad], axis=1)
    for j in range(groups):
        held[0][j, :, base:] = rows
    for batch, leave in batches:
        for copy in batch:
            copy.wait()
        leave.start()
    for _, leave in batches:
        leave.wait()


def pack(q, g, latents, groups, plans):
    tokens = q.shape[0]
    hbm = pl.BlockSpec(memory_space=pl.ANY)
    shapes = []
    for index, (_, pairs) in enumerate(plans):
        width = pairs * PAIR + (LATPAD if index == 0 else 0)
        shapes.append(jax.ShapeDtypeStruct((groups, tokens, width), q.dtype))
    return pl.pallas_call(
        functools.partial(pack_kernel, plans),
        in_specs=[hbm, hbm, pl.BlockSpec(memory_space=pltpu.VMEM)],
        out_specs=[hbm] * len(plans),
        out_shape=shapes,
        scratch_shapes=[pltpu.VMEM(shape.shape, shape.dtype) for shape in shapes]
        + [
            pltpu.SemaphoreType.DMA((2 * groups * len(plans),)),
            pltpu.SemaphoreType.DMA((len(plans), groups)),
        ],
        compiler_params=pltpu.CompilerParams(vmem_limit_bytes=VMEM),
        cost_estimate=pl.CostEstimate(
            flops=0, bytes_accessed=sum(4 * s.size for s in shapes), transcendentals=0
        ),
        name="pack",
    )(q, g, latents)


def unpack_kernel(first, pairs, has_total, with_latents, *refs):
    refs = list(refs)
    if has_total:
        refs.pop(0)
    part_ref, out_ref = refs[:2]
    groups = part_ref.shape[0]
    per_group = out_ref.shape[1] // (groups * QPAIR)
    width = pairs * QPAIR
    sems, held = refs[-2:]
    fetches, copies = [], []
    for j in range(groups):
        at = (j * per_group + first) * QPAIR
        fetches.append(pltpu.make_async_copy(part_ref.at[j], held.at[j], sems.at[0, j]))
        copies.append(
            pltpu.make_async_copy(
                held.at[j, :, :width], out_ref.at[:, at : at + width], sems.at[1, j]
            )
        )
    for fetch in fetches:
        fetch.start()
    for fetch, copy in zip(fetches, copies, strict=True):
        fetch.wait()
        copy.start()
    if with_latents:
        total = held[0, :, width:].astype(jnp.float32)
        for j in range(1, groups):
            total += held[j, :, width:].astype(jnp.float32)
        refs[2][...] = total.T[: LATENT + ROPE].astype(part_ref.dtype)
    for copy in copies:
        copy.wait()


def unpack(total, part, first, pairs, per_group, with_latents):
    groups, tokens, _ = part.shape
    hbm = pl.BlockSpec(memory_space=pl.ANY)
    out_specs = [hbm]
    shapes = [jax.ShapeDtypeStruct((tokens, groups * per_group * QPAIR), part.dtype)]
    if with_latents:
        out_specs.append(pl.BlockSpec(memory_space=pltpu.VMEM))
        shapes.append(jax.ShapeDtypeStruct((LATENT + ROPE, tokens), part.dtype))
    has = total is not None
    return pl.pallas_call(
        functools.partial(unpack_kernel, first, pairs, has, with_latents),
        in_specs=[hbm] * (1 + has),
        out_specs=out_specs,
        out_shape=shapes,
        scratch_shapes=[
            pltpu.SemaphoreType.DMA((2, groups)),
            pltpu.VMEM(part.shape, part.dtype),
        ],
        input_output_aliases={0: 0} if has else {},
        compiler_params=LITTLE,
        cost_estimate=SMALL,
        name="unpack",
    )(*([total] * has + [part]))


def scores_of(head, first, limit):
    q_ref, q_at, g_ref, g_at, key, value = head[:6]
    q = q_ref[first:limit, q_at : q_at + 256]
    g = g_ref[first:limit, g_at : g_at + VDIM]
    scores = dot(key[:limit], q, ((1,), (1,)))
    return scores, dot(value[:limit], g, ((1,), (1,))), q, g


def two_heads(heads, scale, block):
    span = heads[0][4].shape[0]
    steps = [(n, at) for at in reversed(range(span // block)) for n in range(len(heads))]
    dq_rows = [[] for _ in heads]
    ahead = scores_of(heads[0], steps[0][1] * block, (steps[0][1] + 1) * block)
    for number, (n, index) in enumerate(steps):
        first, limit = index * block, (index + 1) * block
        scores, dprobs, q, g = ahead
        if number + 1 < len(steps):
            after_n, after_at = steps[number + 1]
            ahead = scores_of(heads[after_n], after_at * block, (after_at + 1) * block)
        key, dk_ref, dv_ref = heads[n][4], heads[n][6], heads[n][7]
        key_pos = lax.broadcasted_iota(jnp.int32, (block, block), 0)
        query_pos = lax.broadcasted_iota(jnp.int32, (block, block), 1)
        last = jnp.where(key_pos <= query_pos, scores[first:], -jnp.inf)
        scores = jnp.concatenate([scores[:first], last], axis=0) if index else last
        top = jnp.max(scores, axis=0, keepdims=True)
        expo = jnp.exp2((scores - top) * (scale * LOG2E))
        probs = expo * (1.0 / jnp.sum(expo, axis=0, keepdims=True))
        delta = jnp.sum(probs * dprobs, axis=0, keepdims=True)
        dscores = (probs * (dprobs - delta)).astype(jnp.bfloat16)
        dv = dot(probs.astype(jnp.bfloat16), g, ((1,), (0,)))
        dk = dot(dscores, q, ((1,), (0,)))
        if limit == span:
            dv_ref[...] = dv
            dk_ref[...] = dk
        else:
            dv_ref[:limit] += dv
            dk_ref[:limit] += dk
        dq_rows[n].append(dot(dscores, key[:limit], ((0,), (0,))))
    return [jnp.concatenate(rows[::-1], axis=0) for rows in dq_rows]


def attend_kernel(pairs, has_sum, last, *refs):
    refs = list(refs)
    place, lat_ref, w_ref, q_ref = refs[:4]
    rest = refs[4:]
    if pairs == 1:
        q_ref, g_ref = q_ref.at[:, :QPAIR], q_ref.at[:, QPAIR:]
    else:
        g_ref = rest.pop(0)
    sum_in = rest.pop(0) if has_sum else None
    if last:
        dq_ref, keep_ref, send_ref, total, dk0, dv0, dk1, dv1 = rest
        dq_ref, out_ref = dq_ref.at[:, :QPAIR], dq_ref.at[:, QPAIR:]
    else:
        dq_ref, keep_ref, send_ref, out_ref, total, dk0, dv0, dk1, dv1 = rest
    step = pl.program_id(0)
    scale = (NOPE + ROPE) ** (-0.5)
    half = NOPE // 2
    span = lat_ref.shape[0]
    block = min(256, span)
    plain = lat_ref[:, :LATENT]
    rope = lat_ref[:, LATENT:]
    keyval = dot(plain, w_ref[...], ((1,), (0,)))
    lane = lax.broadcasted_iota(jnp.int32, (span, NOPE), 1)
    key0 = jnp.concatenate([keyval[:, :NOPE].astype(jnp.bfloat16), rope], axis=1)
    value0 = keyval[:, NOPE : 2 * NOPE].astype(jnp.bfloat16)
    moved = pltpu.roll(keyval[:, 2 * NOPE : 3 * NOPE], half, 1)
    rope_moved = pltpu.roll(rope.astype(jnp.float32), half, 1)
    key1 = jnp.concatenate(
        [jnp.where(lane < half, 0.0, moved), jnp.where(lane < half, moved, rope_moved)], axis=1
    ).astype(jnp.bfloat16)
    value1 = keyval[:, 3 * NOPE :].astype(jnp.bfloat16)
    dq0, dq1 = two_heads(
        [
            (q_ref, 0, g_ref, 0, key0, value0, dk0, dv0),
            (q_ref, NOPE, g_ref, VDIM, key1, value1, dk1, dv1),
        ],
        scale,
        block,
    )
    dq = jnp.concatenate([dq0[:, :NOPE], dq0[:, NOPE:] + dq1[:, :NOPE], dq1[:, NOPE:]], axis=1)
    dq = (dq * scale).astype(jnp.bfloat16)
    dq_ref[...] = dq
    left = pltpu.roll(dk1[:, :NOPE], half, 1)
    right = pltpu.roll(dk1[:, NOPE:], half, 1)
    dkeyval = jnp.concatenate(
        [
            dk0[:, :NOPE] * scale,
            dv0[...],
            jnp.where(lane < half, left, right) * scale,
            dv1[...],
        ],
        axis=1,
    ).astype(jnp.bfloat16)
    drope = jnp.where(lane < half, (dk0[:, NOPE:] + right) * scale, 0.0)
    back = dot(dkeyval, w_ref[...], ((1,), (1,)))
    dw = dot(plain, dkeyval, ((0,), (0,))).astype(jnp.bfloat16)
    rows = LATENT // 2 // LINE
    for at in range(2 * LINE):
        to = lax.rem(at % LINE - place[1] + LINE, LINE)
        to = pl.ds(pl.multiple_of(to * rows, rows), rows)
        piece = dw[at * rows : (at + 1) * rows]

        @pl.when(place[0] == at // LINE)
        def _():
            keep_ref[to, :] = piece

        @pl.when(place[0] != at // LINE)
        def _():
            send_ref[to, :] = piece

    @pl.when(step == 0)
    def _():
        if has_sum:
            total[:, :LATENT] = back + sum_in[:, :LATENT]
            total[:, LATENT:] = drope + sum_in[:, LATENT:]
        else:
            total[:, :LATENT] = back
            total[:, LATENT:] = drope

    @pl.when(step > 0)
    def _():
        total[:, :LATENT] += back
        total[:, LATENT:] += drope

    @pl.when(step == pl.num_programs(0) - 1)
    def _():
        out_ref[...] = total[...].astype(out_ref.dtype)


def attend(place, lat, lat_block, weight, first, x, pairs, total, last):
    span = lat.shape[0]
    f32, bf16 = jnp.float32, jnp.bfloat16
    whole = lambda j: (0, 0)
    column = lambda j: (0, j)
    specs = [
        pl.BlockSpec(memory_space=pltpu.SMEM),
        pl.BlockSpec((span, LATPAD), lambda j: (0, lat_block)),
        pl.BlockSpec((LATENT, KVPAIR), lambda j: (0, first + j)),
    ]
    args = [place, lat, weight, x]
    if pairs == 1:
        specs.append(pl.BlockSpec((span, PAIR), whole))
    else:
        specs.append(pl.BlockSpec((span, QPAIR), lambda j: (0, pairs * GPAIR // QPAIR + j)))
        specs.append(pl.BlockSpec((span, GPAIR), column))
        args.append(x)
    if total is not None:
        specs.append(pl.BlockSpec((span, LATPAD), whole))
        args.append(total)
    dw_shape = jax.ShapeDtypeStruct((LATENT // 2, pairs * KVPAIR), bf16)
    out_specs = [pl.BlockSpec((LATENT // 2, KVPAIR), column)] * 2
    shapes = [dw_shape, dw_shape]
    if last:
        out_specs = [pl.BlockSpec((span, QPAIR + LATPAD), whole)] + out_specs
        shapes = [jax.ShapeDtypeStruct((span, QPAIR + LATPAD), bf16)] + shapes
    else:
        out_specs = [pl.BlockSpec((span, QPAIR), column)] + out_specs
        shapes = [jax.ShapeDtypeStruct((span, pairs * QPAIR), bf16)] + shapes
        out_specs.append(pl.BlockSpec((span, LATPAD), whole))
        shapes.append(jax.ShapeDtypeStruct((span, LATPAD), f32))
    return pl.pallas_call(
        functools.partial(attend_kernel, pairs, total is not None, last),
        grid=(pairs,),
        in_specs=specs,
        out_specs=out_specs,
        out_shape=shapes,
        scratch_shapes=[
            pltpu.VMEM((span, LATPAD), f32),
            pltpu.VMEM((span, 2 * NOPE), f32),
            pltpu.VMEM((span, VDIM), f32),
            pltpu.VMEM((span, 2 * NOPE), f32),
            pltpu.VMEM((span, VDIM), f32),
        ],
        compiler_params=pltpu.CompilerParams(vmem_limit_bytes=VMEM),
        cost_estimate=pl.CostEstimate(
            flops=pairs * 5_000_000_000, bytes_accessed=pairs * 6_000_000, transcendentals=0
        ),
        name="attend",
    )(*args)


def exchange(x, axis, groups=None):
    return lax.all_to_all(x, axis, split_axis=0, concat_axis=0, tiled=True, axis_index_groups=groups)


def send(x, step):
    slabs = lax.axis_size("dp")
    return lax.ppermute(x, "dp", [(i, step(i)) for i in range(slabs)])


def along(step):
    def to(i):
        near = 2 * LINE
        return i // near * near + ((i // 2 + step) % LINE) * 2 + i % 2

    return to


def add_kernel(*refs):
    *parts, out_ref = refs
    total = parts[0][...].astype(jnp.float32)
    for part in parts[1:]:
        total += part[...].astype(jnp.float32)
    out_ref[...] = total.astype(out_ref.dtype)


def add(*parts):
    cost = pl.CostEstimate(flops=ADD_FLOPS, bytes_accessed=1, transcendentals=0)
    return pl.pallas_call(
        add_kernel, out_shape=parts[0], compiler_params=LITTLE, cost_estimate=cost, name="add"
    )(*parts)


def split_kernel(keep_ref, got_ref, *out_refs):
    total = keep_ref[...].astype(jnp.float32) + got_ref[...].astype(jnp.float32)
    rows = out_refs[0].shape[0]
    for index, out_ref in enumerate(out_refs):
        out_ref[...] = total[index * rows : (index + 1) * rows].astype(out_ref.dtype)


def split(keep, got):
    shape = jax.ShapeDtypeStruct((keep.shape[0] // LINE, keep.shape[1]), keep.dtype)
    shapes = [shape] * LINE
    return pl.pallas_call(
        split_kernel, out_shape=shapes, compiler_params=LITTLE, cost_estimate=SMALL, name="split"
    )(keep, got)


def swap(x):
    return send(x, lambda i: i ^ 1)


def spread(pieces):
    return [pieces[0]] + [send(x, along(k + 1)) for k, x in enumerate(pieces[1:])]


def merge_kernel(count, *refs):
    *parts, out_ref = refs
    at = 0
    for group in (parts[:count], parts[count:]):
        total = group[0][...].astype(jnp.float32)
        for part in group[1:]:
            total += part[...].astype(jnp.float32)
        out_ref[:, at : at + total.shape[1]] = total.astype(out_ref.dtype)
        at += total.shape[1]


def merge(first, second):
    rows = first[0].shape[0]
    shape = jax.ShapeDtypeStruct((rows, first[0].shape[1] + second[0].shape[1]), first[0].dtype)
    kernel = functools.partial(merge_kernel, len(first))
    return pl.pallas_call(
        kernel, out_shape=shape, compiler_params=LITTLE, cost_estimate=SMALL, name="merge"
    )(*first, *second)


def across(part):
    slabs = 4 * LINE
    return send(part, lambda i: (i + slabs // 2) % slabs)


def place_kernel(slabs, place, *refs):
    *parts, out_ref = refs
    rows = parts[0].shape[0]
    for ref, core, k in zip(parts, [0] * LINE + [1] * LINE, 2 * list(range(LINE)), strict=True):
        core = 1 - place[0] if core else place[0]
        at = core * LINE + lax.rem(place[1] - k + LINE, LINE)
        to = pl.ds(pl.multiple_of(at * rows, rows), rows)
        out_ref[to, :] = ref[...].astype(jnp.float32) * (1.0 / slabs)


def place_slabs(place, mine, other):
    vmem = pl.BlockSpec(memory_space=pltpu.VMEM)
    return pl.pallas_call(
        functools.partial(place_kernel, lax.axis_size("dp")),
        in_specs=[pl.BlockSpec(memory_space=pltpu.SMEM)] + [vmem] * (2 * LINE),
        out_specs=vmem,
        out_shape=jax.ShapeDtypeStruct((LATENT, mine[0].shape[1]), jnp.float32),
        compiler_params=LITTLE,
        cost_estimate=SMALL,
        name="place",
    )(place, *mine, *other)


def after(x, *others):
    return lax.optimization_barrier((x,) + others)


def shards(queries, latents, kv_weight, out_grad):
    groups = lax.axis_size("seq")
    tokens = queries.shape[1]
    span = tokens * groups
    per_group = kv_weight.shape[1] // KVPAIR
    late = per_group - EARLY
    q, g, lat = queries[0], out_grad[0], latents[0].T
    me = lax.axis_index("dp")
    place = jnp.stack([me % 2, me // 2 % LINE]).astype(jnp.int32)

    x0, x1 = pack(q, g, lat, groups, ((0, EARLY), (EARLY, late)))
    x0, place = after(x0, place)
    got0 = exchange(x0, "seq")
    x1, got0 = after(x1, got0)
    got1 = exchange(x1, "seq")
    lat = got0.reshape(span, got0.shape[2])
    kv = (place, lat, EARLY * PAIR // LATPAD, kv_weight)
    dq0, keep0, give0, total = attend(*kv, 0, lat, EARLY, None, False)
    back0 = exchange(dq0.reshape(groups, tokens, EARLY * QPAIR), "seq")
    swap0 = swap(give0)
    send1, keep1, give1 = attend(*kv, EARLY, got1.reshape(span, PAIR), late, total, True)
    send1, keep1, give1, keep0, swap0 = after(send1, keep1, give1, keep0, swap0)
    pieces0 = spread(split(keep0, swap0))
    pieces1 = spread(split(keep1, swap(give1)))
    part = merge(pieces0, pieces1)
    other = across(part)
    (query_grad,) = unpack(None, back0, 0, EARLY, per_group, False)
    send1, query_grad, part = after(send1, query_grad, part)
    back1 = exchange(send1.reshape(groups, tokens, QPAIR + LATPAD), "seq")
    line = spread([add(part, other)] * LINE)
    weight_grad = place_slabs(place, line, [swap(x) for x in line])
    query_grad, latent_grad = unpack(query_grad, back1, EARLY, late, per_group, True)
    return (query_grad[None], latent_grad.T[None], weight_grad)


def solution(mesh):
    placed = (P("dp", "seq", None), P("dp", "seq", None), P(None, "seq"), P("dp", "seq", None))
    return jax.shard_map(
        shards,
        mesh=mesh,
        in_specs=placed,
        out_specs=(P("dp", "seq", None), P("dp", "seq", None), P(None, "seq")),
        check_vma=False,
    )
```

```python
import functools

import jax
import jax.numpy as jnp
from jax import lax
from jax.experimental import pallas as pl
from jax.experimental.pallas import tpu as pltpu
from jax.sharding import PartitionSpec as P

NOPE = 128
ROPE = 64
VDIM = 128
LATENT = 512
QPAIR = 2 * (NOPE + ROPE)
GPAIR = 2 * VDIM
PAIR = QPAIR + GPAIR
KVPAIR = 2 * (NOPE + VDIM)
LATPAD = 640
LOG2E = 1.4426950408889634
VMEM = 56 * 1024 * 1024
LITTLE = pltpu.CompilerParams(vmem_limit_bytes=VMEM // 4)
SMALL = pl.CostEstimate(flops=1, bytes_accessed=1, transcendentals=0)
EARLY = 3
LINE = 4
ADD_FLOPS = 40_000_000_000


def dot(a, b, dims):
    return lax.dot_general(a, b, (dims, ((), ())), preferred_element_type=jnp.float32)


def places(pairs):
    return (0, QPAIR) if pairs == 1 else (pairs * GPAIR, 0)


def pack_kernel(plans, q_ref, g_ref, lat_ref, *refs):
    count = len(plans)
    outs, held, sems, sent = refs[:count], refs[count : 2 * count], refs[-2], refs[-1]
    groups = outs[0].shape[0]
    per_group = q_ref.shape[1] // (groups * QPAIR)
    batches, number = [], 0
    for n, (first, pairs) in enumerate(plans):
        for j in range(groups):
            batch = []
            at = j * per_group + first
            q_at, g_at = places(pairs)
            for ref, width, to in ((q_ref, QPAIR, q_at), (g_ref, GPAIR, g_at)):
                batch.append(
                    pltpu.make_async_copy(
                        ref.at[:, at * width : (at + pairs) * width],
                        held[n].at[j, :, to : to + pairs * width],
                        sems.at[number],
                    )
                )
                number += 1
            leave = pltpu.make_async_copy(held[n].at[j], outs[n].at[j], sent.at[n, j])
            batches.append((batch, leave))
    for batch, _ in batches:
        for copy in batch:
            copy.start()
    base = plans[0][1] * PAIR
    rows = lat_ref[...].T
    pad = jnp.zeros((rows.shape[0], LATPAD - rows.shape[1]), rows.dtype)
    rows = jnp.concatenate([rows, pad], axis=1)
    for j in range(groups):
        held[0][j, :, base:] = rows
    for batch, leave in batches:
        for copy in batch:
            copy.wait()
        leave.start()
    for _, leave in batches:
        leave.wait()


def pack(q, g, latents, groups, plans):
    tokens = q.shape[0]
    hbm = pl.BlockSpec(memory_space=pl.ANY)
    shapes = []
    for index, (_, pairs) in enumerate(plans):
        width = pairs * PAIR + (LATPAD if index == 0 else 0)
        shapes.append(jax.ShapeDtypeStruct((groups, tokens, width), q.dtype))
    return pl.pallas_call(
        functools.partial(pack_kernel, plans),
        in_specs=[hbm, hbm, pl.BlockSpec(memory_space=pltpu.VMEM)],
        out_specs=[hbm] * len(plans),
        out_shape=shapes,
        scratch_shapes=[pltpu.VMEM(shape.shape, shape.dtype) for shape in shapes]
        + [
            pltpu.SemaphoreType.DMA((2 * groups * len(plans),)),
            pltpu.SemaphoreType.DMA((len(plans), groups)),
        ],
        compiler_params=pltpu.CompilerParams(vmem_limit_bytes=VMEM),
        cost_estimate=pl.CostEstimate(
            flops=0, bytes_accessed=sum(4 * s.size for s in shapes), transcendentals=0
        ),
        name="pack",
    )(q, g, latents)


def unpack_kernel(first, pairs, has_total, with_latents, *refs):
    refs = list(refs)
    if has_total:
        refs.pop(0)
    part_ref, out_ref = refs[:2]
    groups = part_ref.shape[0]
    per_group = out_ref.shape[1] // (groups * QPAIR)
    width = pairs * QPAIR
    sems, held = refs[-2:]
    fetches, copies = [], []
    for j in range(groups):
        at = (j * per_group + first) * QPAIR
        fetches.append(pltpu.make_async_copy(part_ref.at[j], held.at[j], sems.at[0, j]))
        copies.append(
            pltpu.make_async_copy(
                held.at[j, :, :width], out_ref.at[:, at : at + width], sems.at[1, j]
            )
        )
    for fetch in fetches:
        fetch.start()
    for fetch, copy in zip(fetches, copies, strict=True):
        fetch.wait()
        copy.start()
    if with_latents:
        total = held[0, :, width:].astype(jnp.float32)
        for j in range(1, groups):
            total += held[j, :, width:].astype(jnp.float32)
        refs[2][...] = total.T[: LATENT + ROPE].astype(part_ref.dtype)
    for copy in copies:
        copy.wait()


def unpack(total, part, first, pairs, per_group, with_latents):
    groups, tokens, _ = part.shape
    hbm = pl.BlockSpec(memory_space=pl.ANY)
    out_specs = [hbm]
    shapes = [jax.ShapeDtypeStruct((tokens, groups * per_group * QPAIR), part.dtype)]
    if with_latents:
        out_specs.append(pl.BlockSpec(memory_space=pltpu.VMEM))
        shapes.append(jax.ShapeDtypeStruct((LATENT + ROPE, tokens), part.dtype))
    has = total is not None
    return pl.pallas_call(
        functools.partial(unpack_kernel, first, pairs, has, with_latents),
        in_specs=[hbm] * (1 + has),
        out_specs=out_specs,
        out_shape=shapes,
        scratch_shapes=[
            pltpu.SemaphoreType.DMA((2, groups)),
            pltpu.VMEM(part.shape, part.dtype),
        ],
        input_output_aliases={0: 0} if has else {},
        compiler_params=LITTLE,
        cost_estimate=SMALL,
        name="unpack",
    )(*([total] * has + [part]))


def scores_of(head, first, limit):
    q_ref, q_at, g_ref, g_at, key, value = head[:6]
    q = q_ref[first:limit, q_at : q_at + 256]
    g = g_ref[first:limit, g_at : g_at + VDIM]
    scores = dot(key[:limit], q, ((1,), (1,)))
    return scores, dot(value[:limit], g, ((1,), (1,))), q, g


def two_heads(heads, scale, block):
    span = heads[0][4].shape[0]
    steps = [(n, at) for at in reversed(range(span // block)) for n in range(len(heads))]
    dq_rows = [[] for _ in heads]
    ahead = scores_of(heads[0], steps[0][1] * block, (steps[0][1] + 1) * block)
    for number, (n, index) in enumerate(steps):
        first, limit = index * block, (index + 1) * block
        scores, dprobs, q, g = ahead
        if number + 1 < len(steps):
            after_n, after_at = steps[number + 1]
            ahead = scores_of(heads[after_n], after_at * block, (after_at + 1) * block)
        key, dk_ref, dv_ref = heads[n][4], heads[n][6], heads[n][7]
        key_pos = lax.broadcasted_iota(jnp.int32, (block, block), 0)
        query_pos = lax.broadcasted_iota(jnp.int32, (block, block), 1)
        last = jnp.where(key_pos <= query_pos, scores[first:], -jnp.inf)
        scores = jnp.concatenate([scores[:first], last], axis=0) if index else last
        top = jnp.max(scores, axis=0, keepdims=True)
        expo = jnp.exp2((scores - top) * (scale * LOG2E))
        probs = expo * (1.0 / jnp.sum(expo, axis=0, keepdims=True))
        delta = jnp.sum(probs * dprobs, axis=0, keepdims=True)
        dscores = (probs * (dprobs - delta)).astype(jnp.bfloat16)
        dv = dot(probs.astype(jnp.bfloat16), g, ((1,), (0,)))
        dk = dot(dscores, q, ((1,), (0,)))
        if limit == span:
            dv_ref[...] = dv
            dk_ref[...] = dk
        else:
            dv_ref[:limit] += dv
            dk_ref[:limit] += dk
        dq_rows[n].append(dot(dscores, key[:limit], ((0,), (0,))))
    return [jnp.concatenate(rows[::-1], axis=0) for rows in dq_rows]


def attend_kernel(pairs, has_sum, last, *refs):
    refs = list(refs)
    place, lat_ref, w_ref, q_ref = refs[:4]
    rest = refs[4:]
    if pairs == 1:
        q_ref, g_ref = q_ref.at[:, :QPAIR], q_ref.at[:, QPAIR:]
    else:
        g_ref = rest.pop(0)
    sum_in = rest.pop(0) if has_sum else None
    if last:
        dq_ref, keep_ref, send_ref, total, dk0, dv0, dk1, dv1 = rest
        dq_ref, out_ref = dq_ref.at[:, :QPAIR], dq_ref.at[:, QPAIR:]
    else:
        dq_ref, keep_ref, send_ref, out_ref, total, dk0, dv0, dk1, dv1 = rest
    step = pl.program_id(0)
    scale = (NOPE + ROPE) ** (-0.5)
    half = NOPE // 2
    span = lat_ref.shape[0]
    block = min(256, span)
    plain = lat_ref[:, :LATENT]
    rope = lat_ref[:, LATENT:]
    keyval = dot(plain, w_ref[...], ((1,), (0,)))
    lane = lax.broadcasted_iota(jnp.int32, (span, NOPE), 1)
    key0 = jnp.concatenate([keyval[:, :NOPE].astype(jnp.bfloat16), rope], axis=1)
    value0 = keyval[:, NOPE : 2 * NOPE].astype(jnp.bfloat16)
    moved = pltpu.roll(keyval[:, 2 * NOPE : 3 * NOPE], half, 1)
    rope_moved = pltpu.roll(rope.astype(jnp.float32), half, 1)
    key1 = jnp.concatenate(
        [jnp.where(lane < half, 0.0, moved), jnp.where(lane < half, moved, rope_moved)], axis=1
    ).astype(jnp.bfloat16)
    value1 = keyval[:, 3 * NOPE :].astype(jnp.bfloat16)
    dq0, dq1 = two_heads(
        [
            (q_ref, 0, g_ref, 0, key0, value0, dk0, dv0),
            (q_ref, NOPE, g_ref, VDIM, key1, value1, dk1, dv1),
        ],
        scale,
        block,
    )
    dq = jnp.concatenate([dq0[:, :NOPE], dq0[:, NOPE:] + dq1[:, :NOPE], dq1[:, NOPE:]], axis=1)
    dq = (dq * scale).astype(jnp.bfloat16)
    dq_ref[...] = dq
    left = pltpu.roll(dk1[:, :NOPE], half, 1)
    right = pltpu.roll(dk1[:, NOPE:], half, 1)
    dkeyval = jnp.concatenate(
        [
            dk0[:, :NOPE] * scale,
            dv0[...],
            jnp.where(lane < half, left, right) * scale,
            dv1[...],
        ],
        axis=1,
    ).astype(jnp.bfloat16)
    drope = jnp.where(lane < half, (dk0[:, NOPE:] + right) * scale, 0.0)
    back = dot(dkeyval, w_ref[...], ((1,), (1,)))
    dw = dot(plain, dkeyval, ((0,), (0,))).astype(jnp.bfloat16)
    rows = LATENT // 2 // LINE
    for at in range(2 * LINE):
        to = lax.rem(at % LINE - place[1] + LINE, LINE)
        to = pl.ds(pl.multiple_of(to * rows, rows), rows)
        piece = dw[at * rows : (at + 1) * rows]

        @pl.when(place[0] == at // LINE)
        def _():
            keep_ref[to, :] = piece

        @pl.when(place[0] != at // LINE)
        def _():
            send_ref[to, :] = piece

    @pl.when(step == 0)
    def _():
        if has_sum:
            total[:, :LATENT] = back + sum_in[:, :LATENT]
            total[:, LATENT:] = drope + sum_in[:, LATENT:]
        else:
            total[:, :LATENT] = back
            total[:, LATENT:] = drope

    @pl.when(step > 0)
    def _():
        total[:, :LATENT] += back
        total[:, LATENT:] += drope

    @pl.when(step == pl.num_programs(0) - 1)
    def _():
        out_ref[...] = total[...].astype(out_ref.dtype)


def attend(place, lat, lat_block, weight, first, x, pairs, total, last):
    span = lat.shape[0]
    f32, bf16 = jnp.float32, jnp.bfloat16
    whole = lambda j: (0, 0)
    column = lambda j: (0, j)
    specs = [
        pl.BlockSpec(memory_space=pltpu.SMEM),
        pl.BlockSpec((span, LATPAD), lambda j: (0, lat_block)),
        pl.BlockSpec((LATENT, KVPAIR), lambda j: (0, first + j)),
    ]
    args = [place, lat, weight, x]
    if pairs == 1:
        specs.append(pl.BlockSpec((span, PAIR), whole))
    else:
        specs.append(pl.BlockSpec((span, QPAIR), lambda j: (0, pairs * GPAIR // QPAIR + j)))
        specs.append(pl.BlockSpec((span, GPAIR), column))
        args.append(x)
    if total is not None:
        specs.append(pl.BlockSpec((span, LATPAD), whole))
        args.append(total)
    dw_shape = jax.ShapeDtypeStruct((LATENT // 2, pairs * KVPAIR), bf16)
    out_specs = [pl.BlockSpec((LATENT // 2, KVPAIR), column)] * 2
    shapes = [dw_shape, dw_shape]
    if last:
        out_specs = [pl.BlockSpec((span, QPAIR + LATPAD), whole)] + out_specs
        shapes = [jax.ShapeDtypeStruct((span, QPAIR + LATPAD), bf16)] + shapes
    else:
        out_specs = [pl.BlockSpec((span, QPAIR), column)] + out_specs
        shapes = [jax.ShapeDtypeStruct((span, pairs * QPAIR), bf16)] + shapes
        out_specs.append(pl.BlockSpec((span, LATPAD), whole))
        shapes.append(jax.ShapeDtypeStruct((span, LATPAD), f32))
    return pl.pallas_call(
        functools.partial(attend_kernel, pairs, total is not None, last),
        grid=(pairs,),
        in_specs=specs,
        out_specs=out_specs,
        out_shape=shapes,
        scratch_shapes=[
            pltpu.VMEM((span, LATPAD), f32),
            pltpu.VMEM((span, 2 * NOPE), f32),
            pltpu.VMEM((span, VDIM), f32),
            pltpu.VMEM((span, 2 * NOPE), f32),
            pltpu.VMEM((span, VDIM), f32),
        ],
        compiler_params=pltpu.CompilerParams(vmem_limit_bytes=VMEM * 3 // 4 if last else VMEM),
        cost_estimate=pl.CostEstimate(
            flops=pairs * 5_000_000_000, bytes_accessed=pairs * 6_000_000, transcendentals=0
        ),
        name="attend",
    )(*args)


def exchange(x, axis, groups=None):
    return lax.all_to_all(x, axis, split_axis=0, concat_axis=0, tiled=True, axis_index_groups=groups)


def send(x, step):
    slabs = lax.axis_size("dp")
    return lax.ppermute(x, "dp", [(i, step(i)) for i in range(slabs)])


def along(step):
    def to(i):
        near = 2 * LINE
        return i // near * near + ((i // 2 + step) % LINE) * 2 + i % 2

    return to


def add_kernel(*refs):
    *parts, out_ref = refs
    total = parts[0][...].astype(jnp.float32)
    for part in parts[1:]:
        total += part[...].astype(jnp.float32)
    out_ref[...] = total.astype(out_ref.dtype)


def add(*parts):
    cost = pl.CostEstimate(flops=ADD_FLOPS, bytes_accessed=1, transcendentals=0)
    return pl.pallas_call(
        add_kernel, out_shape=parts[0], compiler_params=LITTLE, cost_estimate=cost, name="add"
    )(*parts)


def split_kernel(keep_ref, got_ref, *out_refs):
    total = keep_ref[...].astype(jnp.float32) + got_ref[...].astype(jnp.float32)
    rows = out_refs[0].shape[0]
    for index, out_ref in enumerate(out_refs):
        out_ref[...] = total[index * rows : (index + 1) * rows].astype(out_ref.dtype)


def split(keep, got):
    shape = jax.ShapeDtypeStruct((keep.shape[0] // LINE, keep.shape[1]), keep.dtype)
    shapes = [shape] * LINE
    return pl.pallas_call(
        split_kernel, out_shape=shapes, compiler_params=LITTLE, cost_estimate=SMALL, name="split"
    )(keep, got)


def swap(x):
    return send(x, lambda i: i ^ 1)


def spread(pieces):
    return [pieces[0]] + [send(x, along(k + 1)) for k, x in enumerate(pieces[1:])]


def merge_kernel(count, *refs):
    *parts, out_ref = refs
    at = 0
    for group in (parts[:count], parts[count:]):
        total = group[0][...].astype(jnp.float32)
        for part in group[1:]:
            total += part[...].astype(jnp.float32)
        out_ref[:, at : at + total.shape[1]] = total.astype(out_ref.dtype)
        at += total.shape[1]


def merge(first, second):
    rows = first[0].shape[0]
    shape = jax.ShapeDtypeStruct((rows, first[0].shape[1] + second[0].shape[1]), first[0].dtype)
    kernel = functools.partial(merge_kernel, len(first))
    return pl.pallas_call(
        kernel, out_shape=shape, compiler_params=LITTLE, cost_estimate=SMALL, name="merge"
    )(*first, *second)


def across(part):
    slabs = 4 * LINE
    return send(part, lambda i: (i + slabs // 2) % slabs)


def place_kernel(slabs, place, *refs):
    *parts, out_ref = refs
    rows = parts[0].shape[0]
    for ref, core, k in zip(parts, [0] * LINE + [1] * LINE, 2 * list(range(LINE)), strict=True):
        core = 1 - place[0] if core else place[0]
        at = core * LINE + lax.rem(place[1] - k + LINE, LINE)
        to = pl.ds(pl.multiple_of(at * rows, rows), rows)
        out_ref[to, :] = ref[...].astype(jnp.float32) * (1.0 / slabs)


def place_slabs(place, mine, other):
    vmem = pl.BlockSpec(memory_space=pltpu.VMEM)
    return pl.pallas_call(
        functools.partial(place_kernel, lax.axis_size("dp")),
        in_specs=[pl.BlockSpec(memory_space=pltpu.SMEM)] + [vmem] * (2 * LINE),
        out_specs=vmem,
        out_shape=jax.ShapeDtypeStruct((LATENT, mine[0].shape[1]), jnp.float32),
        compiler_params=LITTLE,
        cost_estimate=SMALL,
        name="place",
    )(place, *mine, *other)


def after(x, *others):
    return lax.optimization_barrier((x,) + others)


def shards(queries, latents, kv_weight, out_grad):
    groups = lax.axis_size("seq")
    tokens = queries.shape[1]
    span = tokens * groups
    per_group = kv_weight.shape[1] // KVPAIR
    late = per_group - EARLY
    q, g, lat = queries[0], out_grad[0], latents[0].T
    me = lax.axis_index("dp")
    place = jnp.stack([me % 2, me // 2 % LINE]).astype(jnp.int32)

    x0, x1 = pack(q, g, lat, groups, ((0, EARLY), (EARLY, late)))
    x0, place = after(x0, place)
    got0 = exchange(x0, "seq")
    x1, got0 = after(x1, got0)
    got1 = exchange(x1, "seq")
    lat = got0.reshape(span, got0.shape[2])
    kv = (place, lat, EARLY * PAIR // LATPAD, kv_weight)
    dq0, keep0, give0, total = attend(*kv, 0, lat, EARLY, None, False)
    back0 = exchange(dq0.reshape(groups, tokens, EARLY * QPAIR), "seq")
    swap0 = swap(give0)
    send1, keep1, give1 = attend(*kv, EARLY, got1.reshape(span, PAIR), late, total, True)
    send1, keep1, give1, keep0, swap0 = after(send1, keep1, give1, keep0, swap0)
    pieces0 = spread(split(keep0, swap0))
    pieces1 = spread(split(keep1, swap(give1)))
    part = merge(pieces0, pieces1)
    other = across(part)
    (query_grad,) = unpack(None, back0, 0, EARLY, per_group, False)
    send1, query_grad, part = after(send1, query_grad, part)
    back1 = exchange(send1.reshape(groups, tokens, QPAIR + LATPAD), "seq")
    line = spread([add(part, other)] * LINE)
    weight_grad = place_slabs(place, line, [swap(x) for x in line])
    query_grad, latent_grad = unpack(query_grad, back1, EARLY, late, per_group, True)
    return (query_grad[None], latent_grad.T[None], weight_grad)


def solution(mesh):
    placed = (P("dp", "seq", None), P("dp", "seq", None), P(None, "seq"), P("dp", "seq", None))
    return jax.shard_map(
        shards,
        mesh=mesh,
        in_specs=placed,
        out_specs=(P("dp", "seq", None), P("dp", "seq", None), P(None, "seq")),
        check_vma=False,
    )
```
